32 devices in a mesh: cells: 8 (over z, y), bands: 4 (over x, core).
Axes of the slice: x: 2, y: 2, z: 4, core: 2. Of those that a mesh axis runs over, the one named last changes fastest.
Arguments:
- psi: bfloat16 [128, 16, 16, 512], P('cells', None, None, 'bands'), may hold values from -64 to 64
- cell_ham: bfloat16 [64, 729, 729], P('cells'), may hold values from -2 to 2
- proj_table: bfloat16 [4, 8, 16, 729], replicated, may hold values from -0.21875 to 0.21875
- coupling: float32 [4, 16, 16], replicated, may hold values from -0.5 to 0.5
- atom_kind: int32 [16, 2, 2], P('cells'), may hold values from -1 to 3, as said below
Outputs:
- filtered: bfloat16 [128, 16, 16, 512], P('cells', None, None, 'bands')
- correlation: float32 [512, 512], P('cells', 'bands')
The draws below stay inside these ranges and needn't reach their ends.
Inputs may be any that keep to these rules, and one draw needn't show every extreme that they name: `atom_kind`: -1 marks a vertex without an atom; other values name the species.
All inputs are finite; a program needn't handle non-finite values.
Results may differ from the reference program's by a relative error of at most 0.0066.
Values may be sent and summed in bfloat16 or wider, within the bound.
A program may use at most 128 MiB of HBM per device.

```python
import math
import jax
import jax.numpy as jnp
from jax import lax

ORDER = 8
NODES_CELL = 729
CPD = 2
BLOCK = 16
NODES_DEV = 4096
BAND_DEV = 128
NPROJ = 16
KINDS = 4
DEGREE = 3
BLOCKS = 8
CELLS = 64
BANDS = 512


def draw_psi(key, part):
    main_key, node_key, band_key, common_key, loading_key = jax.random.split(key, 5)
    rows_total = BLOCKS * BLOCK
    full_shape = (rows_total, BLOCK, BLOCK, BANDS)
    row_shape = (rows_total, BLOCK, BLOCK, 1)
    owner_index = (jnp.arange(rows_total) // BLOCK).astype(jnp.float32)
    position = (owner_index / max(BLOCKS - 1, 1)).reshape(rows_total, 1, 1, 1)
    randomness = jnp.clip(jax.random.normal(main_key, full_shape, jnp.float32), -6.0, 6.0)
    node_scale = jnp.exp(jax.random.uniform(node_key, row_shape, jnp.float32, math.log(0.2), math.log(2.0)))
    rise_factor = 1.0 + 2.0 * position
    strength = 0.8
    band_scale = jnp.exp(jax.random.uniform(band_key, (BANDS,), jnp.float32, math.log(0.3), math.log(3.0)))
    common_rows = jnp.clip(jax.random.normal(common_key, row_shape, jnp.float32), -4.0, 4.0)
    common_bands = jnp.clip(jax.random.normal(loading_key, (BANDS,), jnp.float32), -3.0, 3.0)
    values = node_scale * jnp.sqrt(rise_factor) * band_scale * (randomness + strength * common_rows * common_bands)
    return jnp.clip(values, -64.0, 64.0).astype(jnp.bfloat16)


def draw_cell_ham(key, part):
    node_index = jnp.arange(ORDER + 1)
    edge_factor = ((node_index == 0) | (node_index == ORDER)).astype(jnp.float32) + 1.0
    multiplicity = (edge_factor[:, None, None] * edge_factor[None, :, None] * edge_factor[None, None, :]).reshape(-1)
    inverse_root = 1.0 / jnp.sqrt(multiplicity)
    spread = 0.45 / math.sqrt(NODES_CELL)

    def one_cell(cell_index):
        cell_key = jax.random.fold_in(key, cell_index)
        diagonal_key, coupling_key = jax.random.split(cell_key)
        diagonal = jax.random.uniform(diagonal_key, (NODES_CELL,), jnp.float32, 0.5, 1.5)
        random_part = jnp.clip(jax.random.normal(coupling_key, (NODES_CELL, NODES_CELL), jnp.float32), -5.0, 5.0)
        symmetric = (random_part + random_part.T) * (spread / math.sqrt(2.0))
        matrix = symmetric * inverse_root[:, None] * inverse_root[None, :] + jnp.diag(diagonal / multiplicity)
        return jnp.clip(matrix, -2.0, 2.0).astype(jnp.bfloat16)
    return lax.map(one_cell, jnp.arange(CELLS))


def draw_atom_kind(key, part):
    presence_key, species_key = jax.random.split(key)
    full_shape = (BLOCKS * CPD, CPD, CPD)
    owner_index = jnp.arange(BLOCKS * CPD, dtype=jnp.int32) // CPD
    threshold = 25 + 70 * owner_index // max(BLOCKS - 1, 1)
    dice_rolls = jax.random.randint(presence_key, full_shape, 0, 100)
    species = jax.random.randint(species_key, full_shape, 0, KINDS)
    chosen = jnp.where(dice_rolls < threshold[:, None, None], species, -1)
    chosen = chosen.at[0, 0, 0].set(-1)
    chosen = chosen.at[BLOCKS * CPD - 1, CPD - 1, CPD - 1].set(KINDS - 1)
    return chosen.astype(jnp.int32)


def centred(rng, dims, width, bound, held_as=jnp.bfloat16):
    return jnp.clip(width * jax.random.normal(rng, dims, jnp.float32), -bound, bound).astype(held_as)


def setup_inputs(seed: int = 0) -> dict:
    splits = jax.random.split(jax.random.key(seed), 6)
    return {
        "psi": draw_psi(jax.random.fold_in(splits[5], 71), 0),
        "cell_ham": draw_cell_ham(jax.random.fold_in(splits[5], 71), 0),
        "proj_table": centred(splits[2], (KINDS, 8, NPROJ, NODES_CELL), NODES_CELL ** -0.5, 0.21875),
        "coupling": centred(splits[3], (KINDS, NPROJ, NPROJ), 0.08, 0.5, jnp.float32),
        "atom_kind": draw_atom_kind(jax.random.fold_in(splits[5], 71), 0),
    }


filter_center = 1.0
highest = lax.Precision.HIGHEST


def cube_root(amount):
    result = 1
    while (result + 1) ** 3 <= amount:
        result = result + 1
    return result


def index_triples(extent):
    return [(along_one, along_two, along_three) for along_one in range(extent) for along_two in range(extent) for along_three in range(extent)]


def fetch_upper(blocks, offsets):
    extended = blocks
    for axis_position, offset in zip((1, 2, 3), offsets):
        neighbour = jnp.roll(extended, -offset, axis=0)
        upper_face = lax.slice_in_dim(neighbour, 0, 1, axis=axis_position)
        extended = jnp.concatenate([extended, upper_face], axis=axis_position)
    return extended


def fold_upper(extended, offsets):
    folded = extended
    for axis_position, offset in zip((1, 2, 3), offsets):
        length = folded.shape[axis_position] - 1
        upper_rim = lax.slice_in_dim(folded, length, length + 1, axis=axis_position)
        arrived = jnp.roll(upper_rim, offset, axis=0)
        lower_face = lax.slice_in_dim(folded, 0, 1, axis=axis_position) + arrived
        remainder = lax.slice_in_dim(folded, 1, length, axis=axis_position)
        folded = jnp.concatenate([lower_face, remainder], axis=axis_position)
    return folded


def corner_values(vertices):
    collected = []
    for cell_one, cell_two, cell_three in index_triples(CPD):
        corners = [vertices[:, cell_one + corner_one, cell_two + corner_two, cell_three + corner_three] for corner_one, corner_two, corner_three in index_triples(2)]
        collected.append(jnp.stack(corners, axis=1))
    return jnp.stack(collected, axis=1)


def corner_fold(corner_parts):
    summed = jnp.zeros((corner_parts.shape[0], CPD + 1, CPD + 1, CPD + 1) + corner_parts.shape[3:], jnp.float32)
    for position, (cell_one, cell_two, cell_three) in enumerate(index_triples(CPD)):
        for corner_position, (corner_one, corner_two, corner_three) in enumerate(index_triples(2)):
            summed = summed.at[:, cell_one + corner_one, cell_two + corner_two, cell_three + corner_three].add(corner_parts[:, position, corner_position])
    return summed


def cell_vectors(extended):
    collected = []
    for cell_one, cell_two, cell_three in index_triples(CPD):
        window = extended[:, cell_one * ORDER:cell_one * ORDER + ORDER + 1, cell_two * ORDER:cell_two * ORDER + ORDER + 1, cell_three * ORDER:cell_three * ORDER + ORDER + 1]
        collected.append(window.reshape(window.shape[0], NODES_CELL, window.shape[-1]))
    return jnp.stack(collected, axis=1)


def assemble(cell_terms):
    edge_nodes = CPD * ORDER + 1
    summed = jnp.zeros((cell_terms.shape[0], edge_nodes, edge_nodes, edge_nodes, cell_terms.shape[-1]), jnp.float32)
    for position, (cell_one, cell_two, cell_three) in enumerate(index_triples(CPD)):
        cube_term = cell_terms[:, position].reshape(cell_terms.shape[0], ORDER + 1, ORDER + 1, ORDER + 1, cell_terms.shape[-1])
        summed = summed.at[:, cell_one * ORDER:cell_one * ORDER + ORDER + 1, cell_two * ORDER:cell_two * ORDER + ORDER + 1, cell_three * ORDER:cell_three * ORDER + ORDER + 1].add(cube_term)
    return summed


def reference(psi, cell_ham, proj_table, coupling, atom_kind):
    grid_side = cube_root(BLOCKS)
    offsets = (1, grid_side, grid_side * grid_side)
    band_groups = BANDS // BAND_DEV
    kinds = atom_kind.reshape(BLOCKS, CPD, CPD, CPD)
    kinds_extended = fetch_upper(kinds, offsets)
    species = jnp.arange(KINDS, dtype=jnp.int32)
    corner_hot = (corner_values(kinds_extended)[..., None] == species).astype(jnp.float32)
    projectors = jnp.einsum('dcok,kopn->dcopn', corner_hot, proj_table.astype(jnp.float32), precision=highest)
    owned_hot = (kinds[..., None] == species).astype(jnp.float32)
    couplings = jnp.einsum('dxyzk,kpq->dxyzpq', owned_hot, coupling, precision=highest)
    hams = cell_ham.reshape(BLOCKS, CPD ** 3, NODES_CELL, NODES_CELL)

    def apply_operator(vectors):
        extended = fetch_upper(vectors, offsets)
        cell_values = cell_vectors(extended).astype(jnp.float32)
        local_part = jnp.einsum('dcij,dcjb->dcib', hams.astype(jnp.float32), cell_values, precision=highest)
        coefficient_parts = jnp.einsum('dcopn,dcnb->dcopb', projectors, cell_values, precision=highest)
        coeffs = fold_upper(corner_fold(coefficient_parts), offsets)
        weights = jnp.einsum('dxyzpq,dxyzqb->dxyzpb', couplings, coeffs, precision=highest).astype(jnp.bfloat16)
        corner_weights = corner_values(fetch_upper(weights, offsets)).astype(jnp.float32)
        projector_part = jnp.einsum('dcopn,dcopb->dcnb', projectors, corner_weights, precision=highest)
        return fold_upper(assemble(local_part + projector_part), offsets)

    def filter_block(start_block):
        previous = start_block
        current = (apply_operator(previous) - filter_center * previous.astype(jnp.float32)).astype(jnp.bfloat16)
        for degree in range(1, DEGREE):
            applied = apply_operator(current)
            upcoming = 2.0 * (applied - filter_center * current.astype(jnp.float32)) - previous.astype(jnp.float32)
            previous, current = current, upcoming.astype(jnp.bfloat16)
        return current

    grouped = psi.reshape(BLOCKS, BLOCK, BLOCK, BLOCK, band_groups, BAND_DEV)
    grouped = jnp.moveaxis(grouped, 4, 0)
    results = lax.map(filter_block, grouped)
    filtered = jnp.moveaxis(results, 0, 4).reshape(BLOCKS * BLOCK, BLOCK, BLOCK, BANDS)
    flat_nodes = filtered.reshape(-1, BANDS)
    inverse_count = 1.0 / (BLOCKS * NODES_DEV)
    correlation = jnp.dot(flat_nodes.T, flat_nodes, preferred_element_type=jnp.float32) * inverse_count
    return filtered, correlation
```

```python
import functools
import jax
import jax.numpy as jnp
from jax import lax
from jax.experimental import pallas as pl
from jax.experimental.pallas import tpu as pltpu
from jax.sharding import PartitionSpec as P

ORDER = 8
CPD = 2
DEGREE = 3
LANES = 128
f32 = jnp.float32
bf16 = jnp.bfloat16

MESSAGES = [(1, 0, 0), (0, 1, 0), (0, 0, 1), (1, 1, 0), (1, 0, 1), (0, 1, 1), (1, 1, 1)]


def cube_root(amount):
    result = 1
    while (result + 1) ** 3 <= amount:
        result = result + 1
    return result


def message_rows(extent, unit):
    starts, start = [], 0
    for m in MESSAGES:
        free = 3 - sum(m)
        rows = max(extent**free * unit, 16)
        starts.append((start, rows))
        start += rows
    return starts, start


def filter_kernel(
    blocks, side, nodes, psi_ref, ham_hbm, table_ref, coupling_ref, kind_ref, out_ref,
    ham, ya, yb, total, vcell, vb, proj, parts, loc, coef, wgt,
    node_out, node_in, vert_out, vert_in,
    node_ssem, node_rsem, vert_ssem, vert_rsem, ham_sem,
):
    block = psi_ref.shape[0]
    edge = block + 1
    pitch = 24
    cells = CPD**3
    cell_edge = ORDER + 1
    kinds = table_ref.shape[0]
    nproj = table_ref.shape[2]
    corners = 8
    corner_span = corners * nproj
    vside = CPD + 1
    me = lax.axis_index("cells")
    offsets = [i * 1 + j * side + k * side * side for i, j, k in MESSAGES]
    ups = [lax.rem(me + o, blocks) for o in offsets]
    downs = [lax.rem(me + blocks - o, blocks) for o in offsets]
    node_rows, _ = message_rows(block, 1)
    vert_rows, _ = message_rows(CPD, nproj)

    ham_copies = [
        pltpu.make_async_copy(ham_hbm.at[c], ham.at[c], ham_sem.at[c]) for c in range(cells)
    ]
    for copy in ham_copies:
        copy.start()

    barrier = pltpu.get_barrier_semaphore()
    for target in ups + downs:
        pl.semaphore_signal(
            barrier, inc=1, device_id={"cells": target}, device_id_type=pl.DeviceIdType.MESH
        )
    pl.semaphore_wait(barrier, len(ups) + len(downs))

    pending = []

    def send(out, arrive, ssem, rsem, ranges, step, targets):
        copies = []
        for m, (start, rows) in enumerate(ranges):
            copy = pltpu.make_async_remote_copy(
                src_ref=out.at[step, pl.ds(start, rows)],
                dst_ref=arrive.at[step, pl.ds(start, rows)],
                send_sem=ssem.at[step, m],
                recv_sem=rsem.at[step, m],
                device_id={"cells": targets[m]},
                device_id_type=pl.DeviceIdType.MESH,
            )
            copy.start()
            copies.append(copy)
        pending.extend(copies)
        return copies

    send_nodes = functools.partial(send, node_out, node_in, node_ssem, node_rsem, node_rows)
    send_verts = functools.partial(send, vert_out, vert_in, vert_ssem, vert_rsem, vert_rows)

    def line(x, y):
        return pl.multiple_of((x * edge + y) * pitch, 8)

    def pack_nodes(field, plane, step):
        (s0, _), (s1, _), (s2, _), (s3, _), (s4, _), (s5, _), (s6, _) = node_rows

        def put(start, value):
            node_out[step, pl.ds(start, block), :] = value.astype(bf16)

        def body(x, carry):
            at = pl.multiple_of(x * block, 16)
            put(s0 + at, field[pl.ds(line(plane, x), block), :])
            put(s1 + at, field[pl.ds(line(x, plane), block), :])
            put(s2 + at, field[pl.ds(line(x, 0) + plane, block, pitch), :])
            return carry

        lax.fori_loop(0, block, body, 0)
        put(s3, field[pl.ds(((plane * edge) + plane) * pitch, block), :])
        put(s4, field[pl.ds((plane * edge) * pitch + plane, block, pitch), :])
        put(s5, field[pl.ds(plane * pitch + plane, block, pitch * edge), :])
        corner = field[pl.ds((plane * edge + plane) * pitch + plane, 1), :]
        put(s6, jnp.broadcast_to(corner, (block, LANES)))

    def unpack_nodes(field, plane, step, add):
        (s0, _), (s1, _), (s2, _), (s3, _), (s4, _), (s5, _), (s6, _) = node_rows

        def put(where, start):
            value = node_in[step, pl.ds(start, block), :].astype(f32)
            if add:
                value = field[where, :] + value
            field[where, :] = value

        def body(x, carry):
            at = pl.multiple_of(x * block, 16)
            put(pl.ds(line(plane, x), block), s0 + at)
            put(pl.ds(line(x, plane), block), s1 + at)
            put(pl.ds(line(x, 0) + plane, block, pitch), s2 + at)
            return carry

        lax.fori_loop(0, block, body, 0)
        put(pl.ds(((plane * edge) + plane) * pitch, block), s3)
        put(pl.ds((plane * edge) * pitch + plane, block, pitch), s4)
        put(pl.ds(plane * pitch + plane, block, pitch * edge), s5)
        where = pl.ds((plane * edge + plane) * pitch + plane, 1)
        value = node_in[step, pl.ds(s6, block), :].astype(f32)[0:1]
        if add:
            value = field[where, :] + value
        field[where, :] = value

    def vertex_places(plane):
        places = []
        for m, (start, _) in zip(MESSAGES, vert_rows):
            spans = [[plane] if fixed else list(range(CPD)) for fixed in m]
            at = start
            for i in spans[0]:
                for j in spans[1]:
                    for k in spans[2]:
                        places.append(((i * vside + j) * vside + k, at))
                        at += nproj
        return places

    def pack_verts(field, plane, step):
        for vertex, at in vertex_places(plane):
            vert_out[step, pl.ds(at, nproj), :] = field[vertex].astype(bf16)

    def unpack_verts(field, plane, step, add):
        for vertex, at in vertex_places(plane):
            value = vert_in[step, pl.ds(at, nproj), :].astype(f32)
            field[vertex] = field[vertex] + value if add else value

    def arrived(copies):
        for copy in copies:
            copy.wait_recv()

    owned = [
        ((i * vside + j) * vside + k, (i * CPD + j) * CPD + k)
        for i in range(CPD) for j in range(CPD) for k in range(CPD)
    ]

    def load_psi(x, carry):
        for y in range(block):
            value = psi_ref[x, y].astype(f32)
            ya[pl.ds(line(x, y), block), :] = value
        return carry

    lax.fori_loop(0, block, load_psi, 0)
    pack_nodes(ya, 0, 0)
    psi_copies = send_nodes(0, downs)
    for vertex, position in owned:
        wgt[vertex] = jnp.full((nproj, LANES), kind_ref[position].astype(f32), f32)
    pack_verts(wgt, 0, 0)
    kind_copies = send_verts(0, downs)

    proj[...] = jnp.zeros_like(proj)
    vcell[...] = jnp.zeros_like(vcell)
    arrived(kind_copies)
    unpack_verts(wgt, CPD, 0, False)

    def place(c):
        ca = c // (CPD * CPD)
        cb = lax.rem(c // CPD, CPD)
        cc = lax.rem(c, CPD)
        return ca, cb, cc

    def corner_vertex(c, o):
        ca, cb, cc = place(c)
        return ((ca + o // 4) * vside + cb + (o // 2) % 2) * vside + cc + o % 2

    def select(c, carry):
        for o in range(corners):
            mark = wgt[corner_vertex(c, o)]
            start = 0
            while start < nodes:
                width = min(LANES, nodes - start)
                chosen = jnp.zeros((nproj, width), f32)
                for q in range(kinds):
                    row = table_ref[q, o, :, start : start + width].astype(f32)
                    chosen = jnp.where(mark[:, :width] == float(q), row, chosen)
                proj[c, o * nproj : (o + 1) * nproj, start : start + width] = chosen.astype(bf16)
                start += LANES
        return carry

    lax.fori_loop(0, cells, select, 0)
    arrived(psi_copies)
    unpack_nodes(ya, block, 0, False)

    def cell_base(c):
        ca, cb, cc = place(c)
        return ((ca * ORDER) * edge + cb * ORDER) * pitch + cc * ORDER

    current, previous = ya, yb
    node_step, vert_step = 1, 1
    for degree in range(DEGREE):

        def gather(c, carry):
            base = cell_base(c)
            for x in range(cell_edge):
                for y in range(cell_edge):
                    at = pl.multiple_of(base + (x * edge + y) * pitch, 8)
                    row = (x * cell_edge + y) * cell_edge
                    vcell[row : row + 8, :] = current[pl.ds(at, 8), :]
                    vcell[row + 8 : row + 9, :] = current[pl.ds(at + 8, 1), :]
            values = vcell[...].astype(bf16)
            vb[c] = values
            parts[c] = jnp.dot(proj[c], values, preferred_element_type=f32)
            return carry

        lax.fori_loop(0, cells, gather, 0)
        coef[...] = jnp.zeros_like(coef)
        for c in range(cells):
            ca, cb, cc = c // 4, (c // 2) % 2, c % 2
            for o in range(corners):
                vertex = ((ca + o // 4) * vside + cb + (o // 2) % 2) * vside + cc + o % 2
                coef[vertex] = coef[vertex] + parts[c, o * nproj : (o + 1) * nproj, :]
        pack_verts(coef, CPD, vert_step)
        coef_copies = send_verts(vert_step, ups)

        if degree == 0:
            for copy in ham_copies:
                copy.wait()

        def multiply(c, carry):
            loc[c, 0:nodes, :] = jnp.dot(ham[c], vb[c, 0:nodes, :], preferred_element_type=f32)
            return carry

        half = cells // 2
        lax.fori_loop(0, half, multiply, 0)
        arrived(coef_copies)
        unpack_verts(coef, 0, vert_step, True)
        for vertex, position in owned:
            kind = kind_ref[position]
            matrix = coupling_ref[jnp.maximum(kind, 0)]
            matrix = jnp.where(kind >= 0, matrix, 0.0)
            value = jnp.dot(
                matrix, coef[vertex], precision=lax.Precision.HIGHEST, preferred_element_type=f32
            )
            wgt[vertex] = value.astype(bf16).astype(f32)
        pack_verts(wgt, 0, vert_step + 1)
        weight_copies = send_verts(vert_step + 1, downs)
        lax.fori_loop(half, cells, multiply, 0)
        total[...] = jnp.zeros_like(total)
        arrived(weight_copies)
        unpack_verts(wgt, CPD, vert_step + 1, False)
        vert_step += 2

        def scatter(c, carry):
            weights = jnp.concatenate([wgt[corner_vertex(c, o)] for o in range(corners)], axis=0)
            term = lax.dot_general(
                proj[c], weights.astype(bf16), (((0,), (0,)), ((), ())), preferred_element_type=f32
            )
            vcell[...] = term
            base = cell_base(c)
            for x in range(cell_edge):
                for y in range(cell_edge):
                    at = pl.multiple_of(base + (x * edge + y) * pitch, 8)
                    row = (x * cell_edge + y) * cell_edge
                    total[pl.ds(at, 8), :] = total[pl.ds(at, 8), :] + (
                        vcell[row : row + 8, :] + loc[c, row : row + 8, :]
                    )
                    total[pl.ds(at + 8, 1), :] = total[pl.ds(at + 8, 1), :] + (
                        vcell[row + 8 : row + 9, :] + loc[c, row + 8 : row + 9, :]
                    )
            return carry

        lax.fori_loop(0, cells, scatter, 0)
        pack_nodes(total, block, node_step)
        fold_copies = send_nodes(node_step, ups)
        arrived(fold_copies)
        unpack_nodes(total, 0, node_step, True)
        node_step += 1
        first, last = degree == 0, degree == DEGREE - 1

        def update(x, carry):
            for y in range(block):
                where = pl.ds(line(x, y), block)
                value = total[where, :] - current[where, :]
                if not first:
                    value = 2.0 * value - previous[where, :]
                value = value.astype(bf16)
                if last:
                    out_ref[x, y] = value
                else:
                    previous[where, :] = value.astype(f32)
            return carry

        lax.fori_loop(0, block, update, 0)
        if not last:
            pack_nodes(previous, 0, node_step)
            field_copies = send_nodes(node_step, downs)
            arrived(field_copies)
            unpack_nodes(previous, block, node_step, False)
            node_step += 1
        current, previous = previous, current

    for copy in pending:
        copy.wait_send()


def run_filter(psi, cell_ham, proj_table, coupling, kinds):
    blocks = lax.axis_size("cells")
    side = cube_root(blocks)
    block = psi.shape[0]
    nodes = cell_ham.shape[-1]
    cells = cell_ham.shape[0]
    padded = -(-nodes // LANES) * LANES
    nproj = proj_table.shape[2]
    corner_span = 8 * nproj
    rows = (block + 1) ** 2 * 24
    node_steps, vert_steps = 2 * DEGREE, 2 * DEGREE + 1
    _, node_buffer = message_rows(block, 1)
    _, vert_buffer = message_rows(CPD, nproj)
    vmem = pl.BlockSpec(memory_space=pltpu.VMEM)
    flops = DEGREE * cells * 2 * LANES * nodes * (nodes + 2 * corner_span)
    return pl.pallas_call(
        functools.partial(filter_kernel, blocks, side, nodes),
        out_shape=jax.ShapeDtypeStruct(psi.shape, bf16),
        in_specs=[
            vmem,
            pl.BlockSpec(memory_space=pl.ANY),
            vmem,
            vmem,
            pl.BlockSpec(memory_space=pltpu.SMEM),
        ],
        out_specs=vmem,
        scratch_shapes=[
            pltpu.VMEM((cells, nodes, nodes), bf16),
            pltpu.VMEM((rows, LANES), f32),
            pltpu.VMEM((rows, LANES), f32),
            pltpu.VMEM((rows, LANES), f32),
            pltpu.VMEM((padded, LANES), f32),
            pltpu.VMEM((cells, padded, LANES), bf16),
            pltpu.VMEM((cells, corner_span, padded), bf16),
            pltpu.VMEM((cells, corner_span, LANES), f32),
            pltpu.VMEM((cells, padded, LANES), f32),
            pltpu.VMEM(((CPD + 1) ** 3, nproj, LANES), f32),
            pltpu.VMEM(((CPD + 1) ** 3, nproj, LANES), f32),
            pltpu.VMEM((node_steps, node_buffer, LANES), bf16),
            pltpu.VMEM((node_steps, node_buffer, LANES), bf16),
            pltpu.VMEM((vert_steps, vert_buffer, LANES), bf16),
            pltpu.VMEM((vert_steps, vert_buffer, LANES), bf16),
            pltpu.SemaphoreType.DMA((node_steps, 7)),
            pltpu.SemaphoreType.DMA((node_steps, 7)),
            pltpu.SemaphoreType.DMA((vert_steps, 7)),
            pltpu.SemaphoreType.DMA((vert_steps, 7)),
            pltpu.SemaphoreType.DMA((cells,)),
        ],
        compiler_params=pltpu.CompilerParams(
            collective_id=0, has_side_effects=True, vmem_limit_bytes=52 * 1024 * 1024
        ),
        cost_estimate=pl.CostEstimate(
            flops=flops, bytes_accessed=cells * nodes * nodes * 2, transcendentals=0
        ),
    )(psi, cell_ham, proj_table, coupling, kinds)


def local(psi, cell_ham, proj_table, coupling, atom_kind):
    blocks = lax.axis_size("cells")
    groups = lax.axis_size("bands")
    band_count = psi.shape[-1]
    filtered = run_filter(psi, cell_ham, proj_table, coupling, atom_kind.reshape(-1))
    flat = filtered.reshape(-1, band_count)
    inverse_count = 1.0 / (flat.shape[0] * blocks)
    share = lax.all_to_all(flat, "bands", 0, 1, tiled=True)
    gram = jnp.einsum("nr,nb->rb", share, share, preferred_element_type=f32) * inverse_count
    bands = band_count * groups
    terms = gram.reshape(blocks, bands // blocks, groups, band_count)
    terms = jnp.transpose(terms, (0, 2, 1, 3)).astype(bf16)
    terms = terms.reshape(blocks * groups, bands // blocks, band_count)
    terms = lax.all_to_all(terms, ("cells", "bands"), 0, 0, tiled=True)
    return (filtered, jnp.sum(terms.astype(f32), axis=0))


def solution(mesh):
    in_specs = (
        P("cells", None, None, "bands"),
        P("cells", None, None),
        P(),
        P(),
        P("cells", None, None),
    )
    out_specs = (P("cells", None, None, "bands"), P("cells", "bands"))
    return jax.shard_map(local, mesh=mesh, in_specs=in_specs, out_specs=out_specs, check_vma=False)
```

```python
import functools
import jax
import jax.numpy as jnp
from jax import lax
from jax.experimental import pallas as pl
from jax.experimental.pallas import tpu as pltpu
from jax.sharding import PartitionSpec as P

ORDER = 8
CPD = 2
DEGREE = 3
LANES = 128
f32 = jnp.float32
bf16 = jnp.bfloat16

MESSAGES = [(1, 0, 0), (0, 1, 0), (0, 0, 1), (1, 1, 0), (1, 0, 1), (0, 1, 1), (1, 1, 1)]


def cube_root(amount):
    result = 1
    while (result + 1) ** 3 <= amount:
        result = result + 1
    return result


def message_rows(extent, unit):
    starts, start = [], 0
    for m in MESSAGES:
        free = 3 - sum(m)
        rows = max(extent**free * unit, 16)
        starts.append((start, rows))
        start += rows
    return starts, start


def filter_kernel(
    blocks, groups, side, nodes, psi_ref, ham_hbm, table_ref, coupling_ref, kind_ref, out_ref, corr_ref,
    ham, ya, yb, total, vcell, vb, proj, parts, loc, coef, wgt,
    node_out, node_in, vert_out, vert_in,
    node_ssem, node_rsem, vert_ssem, vert_rsem, ham_sem,
    inner, faces, slots, wide, gram_out, gram_in, summed, summed_in,
    band_ssem, band_rsem, own_sem, cell_ssem, cell_rsem,
):
    block = psi_ref.shape[0]
    edge = block + 1
    pitch = 24
    cells = CPD**3
    cell_edge = ORDER + 1
    kinds = table_ref.shape[0]
    nproj = table_ref.shape[2]
    corners = 8
    corner_span = corners * nproj
    vside = CPD + 1
    me = lax.axis_index("cells")
    offsets = [i * 1 + j * side + k * side * side for i, j, k in MESSAGES]
    ups = [lax.rem(me + o, blocks) for o in offsets]
    downs = [lax.rem(me + blocks - o, blocks) for o in offsets]
    node_rows, _ = message_rows(block, 1)
    vert_rows, _ = message_rows(CPD, nproj)

    ham_copies = [
        pltpu.make_async_copy(ham_hbm.at[c], ham.at[c], ham_sem.at[c]) for c in range(cells)
    ]
    for copy in ham_copies:
        copy.start()

    barrier = pltpu.get_barrier_semaphore()
    group = lax.axis_index("bands")
    cell_peers = [lax.rem(me + j, blocks) for j in range(1, blocks)]
    band_peers = [lax.rem(group + j, groups) for j in range(1, groups)]
    for target in cell_peers:
        pl.semaphore_signal(
            barrier, inc=1, device_id={"cells": target}, device_id_type=pl.DeviceIdType.MESH
        )
    for target in band_peers:
        pl.semaphore_signal(
            barrier, inc=1, device_id={"bands": target}, device_id_type=pl.DeviceIdType.MESH
        )
    pl.semaphore_wait(barrier, len(cell_peers) + len(band_peers))

    pending = []

    def send(out, arrive, ssem, rsem, ranges, step, targets):
        copies = []
        for m, (start, rows) in enumerate(ranges):
            copy = pltpu.make_async_remote_copy(
                src_ref=out.at[step, pl.ds(start, rows)],
                dst_ref=arrive.at[step, pl.ds(start, rows)],
                send_sem=ssem.at[step, m],
                recv_sem=rsem.at[step, m],
                device_id={"cells": targets[m]},
                device_id_type=pl.DeviceIdType.MESH,
            )
            copy.start()
            copies.append(copy)
        pending.extend(copies)
        return copies

    send_nodes = functools.partial(send, node_out, node_in, node_ssem, node_rsem, node_rows)
    send_verts = functools.partial(send, vert_out, vert_in, vert_ssem, vert_rsem, vert_rows)

    def line(x, y):
        return pl.multiple_of((x * edge + y) * pitch, 8)

    def pack_nodes(field, plane, step):
        (s0, _), (s1, _), (s2, _), (s3, _), (s4, _), (s5, _), (s6, _) = node_rows

        def put(start, value):
            node_out[step, pl.ds(start, block), :] = value.astype(bf16)

        def body(x, carry):
            at = pl.multiple_of(x * block, 16)
            put(s0 + at, field[pl.ds(line(plane, x), block), :])
            put(s1 + at, field[pl.ds(line(x, plane), block), :])
            put(s2 + at, field[pl.ds(line(x, 0) + plane, block, pitch), :])
            return carry

        lax.fori_loop(0, block, body, 0)
        put(s3, field[pl.ds(((plane * edge) + plane) * pitch, block), :])
        put(s4, field[pl.ds((plane * edge) * pitch + plane, block, pitch), :])
        put(s5, field[pl.ds(plane * pitch + plane, block, pitch * edge), :])
        corner = field[pl.ds((plane * edge + plane) * pitch + plane, 1), :]
        put(s6, jnp.broadcast_to(corner, (block, LANES)))

    def unpack_nodes(field, plane, step, add):
        (s0, _), (s1, _), (s2, _), (s3, _), (s4, _), (s5, _), (s6, _) = node_rows

        def put(where, start):
            value = node_in[step, pl.ds(start, block), :].astype(f32)
            if add:
                value = field[where, :] + value
            field[where, :] = value

        def body(x, carry):
            at = pl.multiple_of(x * block, 16)
            put(pl.ds(line(plane, x), block), s0 + at)
            put(pl.ds(line(x, plane), block), s1 + at)
            put(pl.ds(line(x, 0) + plane, block, pitch), s2 + at)
            return carry

        lax.fori_loop(0, block, body, 0)
        put(pl.ds(((plane * edge) + plane) * pitch, block), s3)
        put(pl.ds((plane * edge) * pitch + plane, block, pitch), s4)
        put(pl.ds(plane * pitch + plane, block, pitch * edge), s5)
        where = pl.ds((plane * edge + plane) * pitch + plane, 1)
        value = node_in[step, pl.ds(s6, block), :].astype(f32)[0:1]
        if add:
            value = field[where, :] + value
        field[where, :] = value

    def vertex_places(plane):
        places = []
        for m, (start, _) in zip(MESSAGES, vert_rows):
            spans = [[plane] if fixed else list(range(CPD)) for fixed in m]
            at = start
            for i in spans[0]:
                for j in spans[1]:
                    for k in spans[2]:
                        places.append(((i * vside + j) * vside + k, at))
                        at += nproj
        return places

    def pack_verts(field, plane, step):
        for vertex, at in vertex_places(plane):
            vert_out[step, pl.ds(at, nproj), :] = field[vertex].astype(bf16)

    def unpack_verts(field, plane, step, add):
        for vertex, at in vertex_places(plane):
            value = vert_in[step, pl.ds(at, nproj), :].astype(f32)
            field[vertex] = field[vertex] + value if add else value

    def arrived(copies):
        for copy in copies:
            copy.wait_recv()

    owned = [
        ((i * vside + j) * vside + k, (i * CPD + j) * CPD + k)
        for i in range(CPD) for j in range(CPD) for k in range(CPD)
    ]

    def load_psi(x, carry):
        for y in range(block):
            value = psi_ref[x, y].astype(f32)
            ya[pl.ds(line(x, y), block), :] = value
        return carry

    lax.fori_loop(0, block, load_psi, 0)
    pack_nodes(ya, 0, 0)
    psi_copies = send_nodes(0, downs)
    for vertex, position in owned:
        wgt[vertex] = jnp.full((nproj, LANES), kind_ref[position].astype(f32), f32)
    pack_verts(wgt, 0, 0)
    kind_copies = send_verts(0, downs)

    proj[...] = jnp.zeros_like(proj)
    vcell[...] = jnp.zeros_like(vcell)
    arrived(kind_copies)
    unpack_verts(wgt, CPD, 0, False)

    def place(c):
        ca = c // (CPD * CPD)
        cb = lax.rem(c // CPD, CPD)
        cc = lax.rem(c, CPD)
        return ca, cb, cc

    def corner_vertex(c, o):
        ca, cb, cc = place(c)
        return ((ca + o // 4) * vside + cb + (o // 2) % 2) * vside + cc + o % 2

    def select(c, carry):
        for o in range(corners):
            mark = wgt[corner_vertex(c, o)]
            start = 0
            while start < nodes:
                width = min(LANES, nodes - start)
                chosen = jnp.zeros((nproj, width), f32)
                for q in range(kinds):
                    row = table_ref[q, o, :, start : start + width].astype(f32)
                    chosen = jnp.where(mark[:, :width] == float(q), row, chosen)
                proj[c, o * nproj : (o + 1) * nproj, start : start + width] = chosen.astype(bf16)
                start += LANES
        return carry

    lax.fori_loop(0, cells, select, 0)
    arrived(psi_copies)
    unpack_nodes(ya, block, 0, False)

    def cell_base(c):
        ca, cb, cc = place(c)
        return ((ca * ORDER) * edge + cb * ORDER) * pitch + cc * ORDER

    depth = lax.broadcasted_iota(jnp.int32, (block, LANES), 0)
    share_rows = block**3 // groups
    face_rows = 3 * block * block // groups

    def share(source, start, rows, kind):
        copies = []
        for j, target in enumerate(band_peers):
            copies.append(
                pltpu.make_async_remote_copy(
                    src_ref=source.at[pl.ds(pl.multiple_of(target * rows, 16), rows)],
                    dst_ref=slots.at[group, pl.ds(start, rows)],
                    send_sem=band_ssem.at[kind, j],
                    recv_sem=band_rsem.at[kind, j],
                    device_id={"bands": target},
                    device_id_type=pl.DeviceIdType.MESH,
                )
            )
            copies[-1].start()
        pending.extend(copies)
        own = pltpu.make_async_copy(
            source.at[pl.ds(pl.multiple_of(group * rows, 16), rows)],
            slots.at[group, pl.ds(start, rows)],
            own_sem.at[kind],
        )
        own.start()
        return copies, own

    current, previous = ya, yb
    node_step, vert_step = 1, 1
    for degree in range(DEGREE):

        def gather(c, carry):
            base = cell_base(c)
            for x in range(cell_edge):
                for y in range(cell_edge):
                    at = pl.multiple_of(base + (x * edge + y) * pitch, 8)
                    row = (x * cell_edge + y) * cell_edge
                    vcell[row : row + 8, :] = current[pl.ds(at, 8), :]
                    vcell[row + 8 : row + 9, :] = current[pl.ds(at + 8, 1), :]
            values = vcell[...].astype(bf16)
            vb[c] = values
            parts[c] = jnp.dot(proj[c], values, preferred_element_type=f32)
            return carry

        lax.fori_loop(0, cells, gather, 0)
        coef[...] = jnp.zeros_like(coef)
        for c in range(cells):
            ca, cb, cc = c // 4, (c // 2) % 2, c % 2
            for o in range(corners):
                vertex = ((ca + o // 4) * vside + cb + (o // 2) % 2) * vside + cc + o % 2
                coef[vertex] = coef[vertex] + parts[c, o * nproj : (o + 1) * nproj, :]
        pack_verts(coef, CPD, vert_step)
        coef_copies = send_verts(vert_step, ups)

        if degree == 0:
            for copy in ham_copies:
                copy.wait()

        def multiply(c, carry):
            loc[c, 0:nodes, :] = jnp.dot(ham[c], vb[c, 0:nodes, :], preferred_element_type=f32)
            return carry

        half = cells // 2
        lax.fori_loop(0, half, multiply, 0)
        arrived(coef_copies)
        unpack_verts(coef, 0, vert_step, True)
        for vertex, position in owned:
            kind = kind_ref[position]
            matrix = coupling_ref[jnp.maximum(kind, 0)]
            matrix = jnp.where(kind >= 0, matrix, 0.0)
            value = jnp.dot(
                matrix, coef[vertex], precision=lax.Precision.HIGHEST, preferred_element_type=f32
            )
            wgt[vertex] = value.astype(bf16).astype(f32)
        pack_verts(wgt, 0, vert_step + 1)
        weight_copies = send_verts(vert_step + 1, downs)
        lax.fori_loop(half, cells, multiply, 0)
        total[...] = jnp.zeros_like(total)
        arrived(weight_copies)
        unpack_verts(wgt, CPD, vert_step + 1, False)
        vert_step += 2

        def scatter(c, carry):
            weights = jnp.concatenate([wgt[corner_vertex(c, o)] for o in range(corners)], axis=0)
            term = lax.dot_general(
                proj[c], weights.astype(bf16), (((0,), (0,)), ((), ())), preferred_element_type=f32
            )
            vcell[...] = term
            base = cell_base(c)
            for x in range(cell_edge):
                stores = []
                for y in range(cell_edge):
                    at = pl.multiple_of(base + (x * edge + y) * pitch, 8)
                    row = (x * cell_edge + y) * cell_edge
                    for place_in, rows, size in ((at, row, 8), (at + 8, row + 8, 1)):
                        where = pl.ds(place_in, size)
                        value = vcell[rows : rows + size, :] + loc[c, rows : rows + size, :]
                        stores.append((where, total[where, :] + value))
                for where, value in stores:
                    total[where, :] = value
            return carry

        lax.fori_loop(0, cells, scatter, 0)
        pack_nodes(total, block, node_step)
        fold_copies = send_nodes(node_step, ups)
        first, last = degree == 0, degree == DEGREE - 1

        def advanced(x, y):
            where = pl.ds(line(x, y), block)
            value = total[where, :] - current[where, :]
            if not first:
                value = 2.0 * value - previous[where, :]
            return value.astype(bf16)

        if last:
            def interior(x, carry):
                keep = (depth > 0) & (x > 0)
                for y in range(1, block):
                    value = jnp.where(keep, advanced(x, y).astype(f32), 0.0)
                    inner[pl.ds(pl.multiple_of((x * block + y) * block, 16), block), :] = value.astype(bf16)
                inner[pl.ds(pl.multiple_of(x * block * block, 16), block), :] = jnp.zeros((block, LANES), bf16)
                return carry

            lax.fori_loop(0, block, interior, 0)
            inner_copies = share(inner, 0, share_rows, 0)
        arrived(fold_copies)
        unpack_nodes(total, 0, node_step, True)
        node_step += 1

        def update(x, carry):
            for start in range(0, block, 4):
                stores = [(y, advanced(x, y)) for y in range(start, start + 4)]
                for y, value in stores:
                    if last:
                        out_ref[x, y] = value
                    previous[pl.ds(line(x, y), block), :] = value.astype(f32)
            return carry

        lax.fori_loop(0, block, update, 0)
        if not last:
            pack_nodes(previous, 0, node_step)
            field_copies = send_nodes(node_step, downs)
            arrived(field_copies)
            unpack_nodes(previous, block, node_step, False)
            node_step += 1
        current, previous = previous, current

    lines = block // groups

    def pack_faces(x, carry):
        at = (x // lines) * face_rows + lax.rem(x, lines) * block
        rows = lines * block
        low = current[pl.ds(line(x, 0), block, pitch), :]
        side_face = jnp.where(depth > 0, current[pl.ds(line(x, 0), block), :], 0.0)
        front = jnp.where((depth > 0) & (x > 0), current[pl.ds(line(0, x), block), :], 0.0)
        for part, value in enumerate((low, side_face, front)):
            faces[pl.ds(pl.multiple_of(at + part * rows, 16), block), :] = value.astype(bf16)
        return carry

    lax.fori_loop(0, block, pack_faces, 0)
    face_copies = share(faces, share_rows, face_rows, 1)
    for copies, own in (inner_copies, face_copies):
        own.wait()
        arrived(copies)
    for g in range(groups):
        wide[:, g * LANES : (g + 1) * LANES] = slots[g]
    for g in range(groups):
        product = lax.dot_general(
            wide[:, g * LANES : (g + 1) * LANES], wide[...],
            (((0,), (0,)), ((), ())), preferred_element_type=f32,
        )
        for h in range(groups):
            gram_out[h, g * LANES : (g + 1) * LANES, :] = product[:, h * LANES : (h + 1) * LANES].astype(bf16)
    gram_copies = []
    for j, target in enumerate(band_peers):
        copy = pltpu.make_async_remote_copy(
            src_ref=gram_out.at[target],
            dst_ref=gram_in.at[j],
            send_sem=band_ssem.at[2, j],
            recv_sem=band_rsem.at[2, j],
            device_id={"bands": target},
            device_id_type=pl.DeviceIdType.MESH,
        )
        copy.start()
        gram_copies.append(copy)
    pending.extend(gram_copies)
    arrived(gram_copies)
    share_of = summed.shape[1]
    scale = 1.0 / (blocks * block**3)
    tile = max(share_of, 16)
    for start in range(0, groups * LANES, tile):
        value = gram_out[group, start : start + tile, :].astype(f32)
        for j in range(groups - 1):
            value = value + gram_in[j, start : start + tile, :].astype(f32)
        value = value * scale
        for row in range(0, tile, share_of):
            summed[(start + row) // share_of] = value[row : row + share_of]
    sum_copies = []
    for j, target in enumerate(cell_peers):
        copy = pltpu.make_async_remote_copy(
            src_ref=summed.at[target],
            dst_ref=summed_in.at[j],
            send_sem=cell_ssem.at[j],
            recv_sem=cell_rsem.at[j],
            device_id={"cells": target},
            device_id_type=pl.DeviceIdType.MESH,
        )
        copy.start()
        sum_copies.append(copy)
    pending.extend(sum_copies)
    value = summed[me]
    for j, copy in enumerate(sum_copies):
        copy.wait_recv()
        value = value + summed_in[j]
    corr_ref[...] = value

    for copy in pending:
        copy.wait_send()


def run_filter(psi, cell_ham, proj_table, coupling, kinds):
    blocks = lax.axis_size("cells")
    groups = lax.axis_size("bands")
    side = cube_root(blocks)
    share_of = groups * LANES // blocks
    slot_rows = (psi.shape[0] ** 3 + 3 * psi.shape[0] ** 2) // groups
    block = psi.shape[0]
    nodes = cell_ham.shape[-1]
    cells = cell_ham.shape[0]
    padded = -(-nodes // LANES) * LANES
    nproj = proj_table.shape[2]
    corner_span = 8 * nproj
    rows = (block + 1) ** 2 * 24
    node_steps, vert_steps = 2 * DEGREE, 2 * DEGREE + 1
    _, node_buffer = message_rows(block, 1)
    _, vert_buffer = message_rows(CPD, nproj)
    vmem = pl.BlockSpec(memory_space=pltpu.VMEM)
    flops = DEGREE * cells * 2 * LANES * nodes * (nodes + 2 * corner_span)
    return pl.pallas_call(
        functools.partial(filter_kernel, blocks, groups, side, nodes),
        out_shape=(
            jax.ShapeDtypeStruct(psi.shape, bf16),
            jax.ShapeDtypeStruct((share_of, LANES), f32),
        ),
        in_specs=[
            vmem,
            pl.BlockSpec(memory_space=pl.ANY),
            vmem,
            vmem,
            pl.BlockSpec(memory_space=pltpu.SMEM),
        ],
        out_specs=(vmem, vmem),
        scratch_shapes=[
            pltpu.VMEM((cells, nodes, nodes), bf16),
            pltpu.VMEM((rows, LANES), f32),
            pltpu.VMEM((rows, LANES), f32),
            pltpu.VMEM((rows, LANES), f32),
            pltpu.VMEM((padded, LANES), f32),
            pltpu.VMEM((cells, padded, LANES), bf16),
            pltpu.VMEM((cells, corner_span, padded), bf16),
            pltpu.VMEM((cells, corner_span, LANES), f32),
            pltpu.VMEM((cells, padded, LANES), f32),
            pltpu.VMEM(((CPD + 1) ** 3, nproj, LANES), f32),
            pltpu.VMEM(((CPD + 1) ** 3, nproj, LANES), f32),
            pltpu.VMEM((node_steps, node_buffer, LANES), bf16),
            pltpu.VMEM((node_steps, node_buffer, LANES), bf16),
            pltpu.VMEM((vert_steps, vert_buffer, LANES), bf16),
            pltpu.VMEM((vert_steps, vert_buffer, LANES), bf16),
            pltpu.SemaphoreType.DMA((node_steps, 7)),
            pltpu.SemaphoreType.DMA((node_steps, 7)),
            pltpu.SemaphoreType.DMA((vert_steps, 7)),
            pltpu.SemaphoreType.DMA((vert_steps, 7)),
            pltpu.SemaphoreType.DMA((cells,)),
            pltpu.VMEM((block**3, LANES), bf16),
            pltpu.VMEM((3 * block**2, LANES), bf16),
            pltpu.VMEM((groups, slot_rows, LANES), bf16),
            pltpu.VMEM((slot_rows, groups * LANES), bf16),
            pltpu.VMEM((groups, groups * LANES, LANES), bf16),
            pltpu.VMEM((groups - 1, groups * LANES, LANES), bf16),
            pltpu.VMEM((blocks, share_of, LANES), f32),
            pltpu.VMEM((blocks - 1, share_of, LANES), f32),
            pltpu.SemaphoreType.DMA((3, groups - 1)),
            pltpu.SemaphoreType.DMA((3, groups - 1)),
            pltpu.SemaphoreType.DMA((2,)),
            pltpu.SemaphoreType.DMA((blocks - 1,)),
            pltpu.SemaphoreType.DMA((blocks - 1,)),
        ],
        compiler_params=pltpu.CompilerParams(
            collective_id=0, has_side_effects=True, vmem_limit_bytes=52 * 1024 * 1024
        ),
        cost_estimate=pl.CostEstimate(
            flops=flops, bytes_accessed=cells * nodes * nodes * 2, transcendentals=0
        ),
    )(psi, cell_ham, proj_table, coupling, kinds)


def local(psi, cell_ham, proj_table, coupling, atom_kind):
    return run_filter(psi, cell_ham, proj_table, coupling, atom_kind.reshape(-1))


def solution(mesh):
    in_specs = (
        P("cells", None, None, "bands"),
        P("cells", None, None),
        P(),
        P(),
        P("cells", None, None),
    )
    out_specs = (P("cells", None, None, "bands"), P("cells", "bands"))
    return jax.shard_map(local, mesh=mesh, in_specs=in_specs, out_specs=out_specs, check_vma=False)
```

```python
import functools
import jax
import jax.numpy as jnp
from jax import lax
from jax.experimental import pallas as pl
from jax.experimental.pallas import tpu as pltpu
from jax.sharding import PartitionSpec as P

ORDER = 8
CPD = 2
DEGREE = 3
LANES = 128
f32 = jnp.float32
bf16 = jnp.bfloat16

MESSAGES = [(1, 0, 0), (0, 1, 0), (0, 0, 1), (1, 1, 0), (1, 0, 1), (0, 1, 1), (1, 1, 1)]


def cube_root(amount):
    result = 1
    while (result + 1) ** 3 <= amount:
        result = result + 1
    return result


def message_rows(extent, unit):
    starts, start = [], 0
    for m in MESSAGES:
        free = 3 - sum(m)
        rows = max(extent**free * unit, 16)
        starts.append((start, rows))
        start += rows
    return starts, start


def filter_kernel(
    blocks, groups, side, nodes, psi_ref, ham_hbm, table_ref, coupling_ref, kind_ref, out_ref, corr_ref,
    ham, ya, yb, total, vcell, vb, proj, parts, loc, coef, wgt,
    node_out, node_in, vert_out, vert_in,
    node_ssem, node_rsem, vert_ssem, vert_rsem, ham_sem,
    raw, stage, projt, inner, faces, slots, wide, gram_out, gram_in, summed, summed_in,
    band_ssem, band_rsem, own_sem, cell_ssem, cell_rsem,
):
    block = psi_ref.shape[0]
    edge = block + 1
    pitch = 24
    cells = CPD**3
    cell_edge = ORDER + 1
    kinds = table_ref.shape[0]
    nproj = table_ref.shape[2]
    corners = 8
    corner_span = corners * nproj
    vside = CPD + 1
    me = lax.axis_index("cells")
    offsets = [i * 1 + j * side + k * side * side for i, j, k in MESSAGES]
    ups = [lax.rem(me + o, blocks) for o in offsets]
    downs = [lax.rem(me + blocks - o, blocks) for o in offsets]
    node_rows, _ = message_rows(block, 1)
    vert_rows, _ = message_rows(CPD, nproj)

    ham_copy = pltpu.make_async_copy(ham_hbm, raw, ham_sem.at[0])
    ham_copy.start()

    barrier = pltpu.get_barrier_semaphore()
    group = lax.axis_index("bands")
    cell_peers = [lax.rem(me + j, blocks) for j in range(1, blocks)]
    band_peers = [lax.rem(group + j, groups) for j in range(1, groups)]
    for target in cell_peers:
        pl.semaphore_signal(
            barrier, inc=1, device_id={"cells": target}, device_id_type=pl.DeviceIdType.MESH
        )
    for target in band_peers:
        pl.semaphore_signal(
            barrier, inc=1, device_id={"bands": target}, device_id_type=pl.DeviceIdType.MESH
        )
    pl.semaphore_wait(barrier, len(cell_peers) + len(band_peers))

    pending = []

    def send(out, arrive, ssem, rsem, ranges, step, targets, chosen=range(7)):
        copies = []
        for m in chosen:
            start, rows = ranges[m]
            copy = pltpu.make_async_remote_copy(
                src_ref=out.at[step, pl.ds(start, rows)],
                dst_ref=arrive.at[step, pl.ds(start, rows)],
                send_sem=ssem.at[step, m],
                recv_sem=rsem.at[step, m],
                device_id={"cells": targets[m]},
                device_id_type=pl.DeviceIdType.MESH,
            )
            copy.start()
            copies.append(copy)
        pending.extend(copies)
        return copies

    send_nodes = functools.partial(send, node_out, node_in, node_ssem, node_rsem, node_rows)
    send_verts = functools.partial(send, vert_out, vert_in, vert_ssem, vert_rsem, vert_rows)

    def line(x, y):
        return pl.multiple_of((x * edge + y) * pitch, 8)

    def pack_nodes(field, plane, step, with_x=True, without_x=True):
        (s0, _), (s1, _), (s2, _), (s3, _), (s4, _), (s5, _), (s6, _) = node_rows

        def put(start, value):
            node_out[step, pl.ds(start, block), :] = value.astype(bf16)

        def body(x, carry):
            at = pl.multiple_of(x * block, 16)
            if with_x:
                put(s0 + at, field[pl.ds(line(plane, x), block), :])
            if without_x:
                put(s1 + at, field[pl.ds(line(x, plane), block), :])
                put(s2 + at, field[pl.ds(line(x, 0) + plane, block, pitch), :])
            return carry

        lax.fori_loop(0, block, body, 0, unroll=4)
        if with_x:
            put(s3, field[pl.ds(((plane * edge) + plane) * pitch, block), :])
            put(s4, field[pl.ds((plane * edge) * pitch + plane, block, pitch), :])
            corner = field[pl.ds((plane * edge + plane) * pitch + plane, 1), :]
            put(s6, jnp.broadcast_to(corner, (block, LANES)))
        if without_x:
            put(s5, field[pl.ds(plane * pitch + plane, block, pitch * edge), :])

    def unpack_nodes(field, plane, step, add):
        (s0, _), (s1, _), (s2, _), (s3, _), (s4, _), (s5, _), (s6, _) = node_rows

        def put(where, start):
            value = node_in[step, pl.ds(start, block), :].astype(f32)
            if add:
                value = field[where, :] + value
            field[where, :] = value

        def body(x, carry):
            at = pl.multiple_of(x * block, 16)
            put(pl.ds(line(plane, x), block), s0 + at)
            put(pl.ds(line(x, plane), block), s1 + at)
            put(pl.ds(line(x, 0) + plane, block, pitch), s2 + at)
            return carry

        lax.fori_loop(0, block, body, 0)
        put(pl.ds(((plane * edge) + plane) * pitch, block), s3)
        put(pl.ds((plane * edge) * pitch + plane, block, pitch), s4)
        put(pl.ds(plane * pitch + plane, block, pitch * edge), s5)
        where = pl.ds((plane * edge + plane) * pitch + plane, 1)
        value = node_in[step, pl.ds(s6, block), :].astype(f32)[0:1]
        if add:
            value = field[where, :] + value
        field[where, :] = value

    def vertex_places(plane):
        places = []
        for m, (start, _) in zip(MESSAGES, vert_rows):
            spans = [[plane] if fixed else list(range(CPD)) for fixed in m]
            at = start
            for i in spans[0]:
                for j in spans[1]:
                    for k in spans[2]:
                        places.append(((i * vside + j) * vside + k, at))
                        at += nproj
        return places

    def pack_verts(field, plane, step):
        for vertex, at in vertex_places(plane):
            vert_out[step, pl.ds(at, nproj), :] = field[vertex].astype(bf16)

    def unpack_verts(field, plane, step, add):
        for vertex, at in vertex_places(plane):
            value = vert_in[step, pl.ds(at, nproj), :].astype(f32)
            field[vertex] = field[vertex] + value if add else value

    def arrived(copies):
        for copy in copies:
            copy.wait_recv()

    owned = [
        ((i * vside + j) * vside + k, (i * CPD + j) * CPD + k)
        for i in range(CPD) for j in range(CPD) for k in range(CPD)
    ]

    def load_psi(x, carry):
        for y in range(block):
            value = psi_ref[x, y].astype(f32)
            ya[pl.ds(line(x, y), block), :] = value
        return carry

    lax.fori_loop(0, block, load_psi, 0)
    pack_nodes(ya, 0, 0)
    psi_copies = send_nodes(0, downs)
    for vertex, position in owned:
        wgt[vertex] = jnp.full((nproj, LANES), kind_ref[position].astype(f32), f32)
    pack_verts(wgt, 0, 0)
    kind_copies = send_verts(0, downs)

    full, tail = nodes // 16, nodes % 16
    chunks = [(n, start, min(LANES, nodes - start)) for n, start in enumerate(range(0, nodes, LANES))]

    def relayout(t, rows):
        for r in range(rows):
            value = raw[t * 16 + r].astype(f32)
            for n, start, width in chunks:
                stage[n, r * cells : (r + 1) * cells, 0:width] = value[:, start : start + width]
        for c in range(cells):
            for n, start, _ in chunks:
                value = stage[n, pl.ds(c, 16, cells), :].astype(bf16)
                ham[c, pl.ds(pl.multiple_of(t * 16, 16), 16), start : start + LANES] = value

    def relayout_body(t, carry):
        relayout(t, 16)
        return carry

    early = full * 2 // 3
    stage[...] = jnp.zeros_like(stage)
    ham_copy.wait()
    lax.fori_loop(0, early, relayout_body, 0)
    proj[...] = jnp.zeros_like(proj)
    vcell[...] = jnp.zeros_like(vcell)
    arrived(kind_copies)
    unpack_verts(wgt, CPD, 0, False)

    def place(c):
        ca = c // (CPD * CPD)
        cb = lax.rem(c // CPD, CPD)
        cc = lax.rem(c, CPD)
        return ca, cb, cc

    def corner_vertex(c, o):
        ca, cb, cc = place(c)
        return ((ca + o // 4) * vside + cb + (o // 2) % 2) * vside + cc + o % 2

    def select(c, carry):
        for o in range(corners):
            mark = wgt[corner_vertex(c, o)]
            start = 0
            while start < nodes:
                width = min(LANES, nodes - start)
                chosen = jnp.zeros((nproj, width), f32)
                for q in range(kinds):
                    row = table_ref[q, o, :, start : start + width].astype(f32)
                    chosen = jnp.where(mark[:, :width] == float(q), row, chosen)
                proj[c, o * nproj : (o + 1) * nproj, start : start + width] = chosen.astype(bf16)
                start += LANES
        projt[c] = jnp.transpose(proj[c].astype(f32)).astype(bf16)
        return carry

    lax.fori_loop(0, cells, select, 0)
    arrived(psi_copies)
    unpack_nodes(ya, block, 0, False)

    def cell_base(c):
        ca, cb, cc = place(c)
        return ((ca * ORDER) * edge + cb * ORDER) * pitch + cc * ORDER

    depth = lax.broadcasted_iota(jnp.int32, (block, LANES), 0)
    share_rows = block**3 // groups
    face_rows = 3 * block * block // groups

    def share(source, start, rows, kind):
        copies = []
        for j, target in enumerate(band_peers):
            copies.append(
                pltpu.make_async_remote_copy(
                    src_ref=source.at[pl.ds(pl.multiple_of(target * rows, 16), rows)],
                    dst_ref=slots.at[group, pl.ds(start, rows)],
                    send_sem=band_ssem.at[kind, j],
                    recv_sem=band_rsem.at[kind, j],
                    device_id={"bands": target},
                    device_id_type=pl.DeviceIdType.MESH,
                )
            )
            copies[-1].start()
        pending.extend(copies)
        own = pltpu.make_async_copy(
            source.at[pl.ds(pl.multiple_of(group * rows, 16), rows)],
            slots.at[group, pl.ds(start, rows)],
            own_sem.at[kind],
        )
        own.start()
        return copies, own

    current, previous = ya, yb
    node_step, vert_step = 1, 1
    for degree in range(DEGREE):

        def gather(c, carry):
            base = cell_base(c)
            for x in range(cell_edge):
                for y in range(cell_edge):
                    at = pl.multiple_of(base + (x * edge + y) * pitch, 8)
                    row = (x * cell_edge + y) * cell_edge
                    vcell[row : row + 8, :] = current[pl.ds(at, 8), :]
                    vcell[row + 8 : row + 9, :] = current[pl.ds(at + 8, 1), :]
            values = vcell[...].astype(bf16)
            vb[c] = values
            parts[c] = jnp.dot(proj[c], values, preferred_element_type=f32)
            return carry

        lax.fori_loop(0, cells, gather, 0, unroll=2)
        coef[...] = jnp.zeros_like(coef)
        for c in range(cells):
            ca, cb, cc = c // 4, (c // 2) % 2, c % 2
            for o in range(corners):
                vertex = ((ca + o // 4) * vside + cb + (o // 2) % 2) * vside + cc + o % 2
                coef[vertex] = coef[vertex] + parts[c, o * nproj : (o + 1) * nproj, :]
        pack_verts(coef, CPD, vert_step)
        coef_copies = send_verts(vert_step, ups)

        if degree == 0:
            lax.fori_loop(early, full, relayout_body, 0)
            if tail:
                stage[:, tail * cells :, :] = jnp.zeros((len(chunks), (16 - tail) * cells, LANES), f32)
                relayout(full, tail)

        def multiply(c, carry):
            loc[c, 0 : ham.shape[1], :] = jnp.dot(ham[c], vb[c], preferred_element_type=f32)
            return carry

        half = cells // 2
        lax.fori_loop(0, half, multiply, 0)
        arrived(coef_copies)
        unpack_verts(coef, 0, vert_step, True)
        for vertex, position in owned:
            kind = kind_ref[position]
            matrix = coupling_ref[jnp.maximum(kind, 0)]
            matrix = jnp.where(kind >= 0, matrix, 0.0)
            value = jnp.dot(
                matrix, coef[vertex], precision=lax.Precision.HIGHEST, preferred_element_type=f32
            )
            wgt[vertex] = value.astype(bf16).astype(f32)
        pack_verts(wgt, 0, vert_step + 1)
        weight_copies = send_verts(vert_step + 1, downs)
        lax.fori_loop(half, cells, multiply, 0)
        total[...] = jnp.zeros_like(total)
        arrived(weight_copies)
        unpack_verts(wgt, CPD, vert_step + 1, False)
        vert_step += 2

        def scatter(c, carry):
            weights = jnp.concatenate([wgt[corner_vertex(c, o)] for o in range(corners)], axis=0)
            vcell[...] = jnp.dot(projt[c], weights.astype(bf16), preferred_element_type=f32)
            base = cell_base(c)
            for x in range(cell_edge):
                stores = []
                for y in range(cell_edge):
                    at = pl.multiple_of(base + (x * edge + y) * pitch, 8)
                    row = (x * cell_edge + y) * cell_edge
                    for place_in, rows, size in ((at, row, 8), (at + 8, row + 8, 1)):
                        where = pl.ds(place_in, size)
                        value = vcell[rows : rows + size, :] + loc[c, rows : rows + size, :]
                        stores.append((where, total[where, :] + value))
                for where, value in stores:
                    total[where, :] = value
            return carry

        lax.fori_loop(half, cells, scatter, 0)
        pack_nodes(total, block, node_step, without_x=False)
        fold_copies = send_nodes(node_step, ups, [m for m in range(7) if MESSAGES[m][0]])
        lax.fori_loop(0, half, scatter, 0)
        pack_nodes(total, block, node_step, with_x=False)
        fold_copies += send_nodes(node_step, ups, [m for m in range(7) if not MESSAGES[m][0]])
        first, last = degree == 0, degree == DEGREE - 1

        def advanced(x, y):
            where = pl.ds(line(x, y), block)
            value = total[where, :] - current[where, :]
            if not first:
                value = 2.0 * value - previous[where, :]
            return value.astype(bf16)

        if last:
            def interior(x, carry):
                keep = (depth > 0) & (x > 0)
                for y in range(1, block):
                    value = jnp.where(keep, advanced(x, y).astype(f32), 0.0)
                    inner[pl.ds(pl.multiple_of((x * block + y) * block, 16), block), :] = value.astype(bf16)
                inner[pl.ds(pl.multiple_of(x * block * block, 16), block), :] = jnp.zeros((block, LANES), bf16)
                return carry

            lax.fori_loop(0, block, interior, 0)
            inner_copies = share(inner, 0, share_rows, 0)
        arrived(fold_copies)
        unpack_nodes(total, 0, node_step, True)
        node_step += 1

        def update(x, carry):
            for start in range(0, block, 4):
                stores = [(y, advanced(x, y)) for y in range(start, start + 4)]
                for y, value in stores:
                    if last:
                        out_ref[x, y] = value
                    previous[pl.ds(line(x, y), block), :] = value.astype(f32)
            return carry

        lax.fori_loop(0, block, update, 0)
        if not last:
            pack_nodes(previous, 0, node_step)
            field_copies = send_nodes(node_step, downs)
            arrived(field_copies)
            unpack_nodes(previous, block, node_step, False)
            node_step += 1
        current, previous = previous, current

    lines = block // groups

    def pack_faces(x, carry):
        at = (x // lines) * face_rows + lax.rem(x, lines) * block
        rows = lines * block
        low = current[pl.ds(line(x, 0), block, pitch), :]
        side_face = jnp.where(depth > 0, current[pl.ds(line(x, 0), block), :], 0.0)
        front = jnp.where((depth > 0) & (x > 0), current[pl.ds(line(0, x), block), :], 0.0)
        for part, value in enumerate((low, side_face, front)):
            faces[pl.ds(pl.multiple_of(at + part * rows, 16), block), :] = value.astype(bf16)
        return carry

    lax.fori_loop(0, block, pack_faces, 0)
    face_copies = share(faces, share_rows, face_rows, 1)
    for copies, own in (inner_copies, face_copies):
        own.wait()
        arrived(copies)
    for g in range(groups):
        wide[:, g * LANES : (g + 1) * LANES] = slots[g]
    for g in range(groups):
        product = lax.dot_general(
            wide[:, g * LANES : (g + 1) * LANES], wide[...],
            (((0,), (0,)), ((), ())), preferred_element_type=f32,
        )
        for h in range(groups):
            gram_out[h, g * LANES : (g + 1) * LANES, :] = product[:, h * LANES : (h + 1) * LANES].astype(bf16)
    gram_copies = []
    for j, target in enumerate(band_peers):
        copy = pltpu.make_async_remote_copy(
            src_ref=gram_out.at[target],
            dst_ref=gram_in.at[j],
            send_sem=band_ssem.at[2, j],
            recv_sem=band_rsem.at[2, j],
            device_id={"bands": target},
            device_id_type=pl.DeviceIdType.MESH,
        )
        copy.start()
        gram_copies.append(copy)
    pending.extend(gram_copies)
    arrived(gram_copies)
    share_of = summed.shape[1]
    scale = 1.0 / (blocks * block**3)
    tile = max(share_of, 16)
    for start in range(0, groups * LANES, tile):
        value = gram_out[group, start : start + tile, :].astype(f32)
        for j in range(groups - 1):
            value = value + gram_in[j, start : start + tile, :].astype(f32)
        value = value * scale
        for row in range(0, tile, share_of):
            summed[(start + row) // share_of] = value[row : row + share_of].astype(summed.dtype)
    sum_copies = []
    for j, target in enumerate(cell_peers):
        copy = pltpu.make_async_remote_copy(
            src_ref=summed.at[target],
            dst_ref=summed_in.at[j],
            send_sem=cell_ssem.at[j],
            recv_sem=cell_rsem.at[j],
            device_id={"cells": target},
            device_id_type=pl.DeviceIdType.MESH,
        )
        copy.start()
        sum_copies.append(copy)
    pending.extend(sum_copies)
    value = summed[me].astype(f32)
    for j, copy in enumerate(sum_copies):
        copy.wait_recv()
        value = value + summed_in[j].astype(f32)
    corr_ref[...] = value

    for copy in pending:
        copy.wait_send()


def run_filter(psi, cell_ham, proj_table, coupling, kinds):
    blocks = lax.axis_size("cells")
    groups = lax.axis_size("bands")
    side = cube_root(blocks)
    share_of = groups * LANES // blocks
    sum_type = f32 if share_of % 16 else bf16
    slot_rows = (psi.shape[0] ** 3 + 3 * psi.shape[0] ** 2) // groups
    block = psi.shape[0]
    nodes = cell_ham.shape[-1]
    cells = cell_ham.shape[0]
    padded = -(-nodes // LANES) * LANES
    nproj = proj_table.shape[2]
    corner_span = 8 * nproj
    rows = (block + 1) ** 2 * 24
    node_steps, vert_steps = 2 * DEGREE, 2 * DEGREE + 1
    _, node_buffer = message_rows(block, 1)
    _, vert_buffer = message_rows(CPD, nproj)
    vmem = pl.BlockSpec(memory_space=pltpu.VMEM)
    flops = DEGREE * cells * 2 * LANES * nodes * (nodes + 2 * corner_span)
    return pl.pallas_call(
        functools.partial(filter_kernel, blocks, groups, side, nodes),
        out_shape=(
            jax.ShapeDtypeStruct(psi.shape, bf16),
            jax.ShapeDtypeStruct((share_of, LANES), f32),
        ),
        in_specs=[
            vmem,
            pl.BlockSpec(memory_space=pl.ANY),
            vmem,
            vmem,
            pl.BlockSpec(memory_space=pltpu.SMEM),
        ],
        out_specs=(vmem, vmem),
        scratch_shapes=[
            pltpu.VMEM((cells, -(-nodes // 16) * 16, padded), bf16),
            pltpu.VMEM((rows, LANES), f32),
            pltpu.VMEM((rows, LANES), f32),
            pltpu.VMEM((rows, LANES), f32),
            pltpu.VMEM((padded, LANES), f32),
            pltpu.VMEM((cells, padded, LANES), bf16),
            pltpu.VMEM((cells, corner_span, padded), bf16),
            pltpu.VMEM((cells, corner_span, LANES), f32),
            pltpu.VMEM((cells, padded, LANES), f32),
            pltpu.VMEM(((CPD + 1) ** 3, nproj, LANES), f32),
            pltpu.VMEM(((CPD + 1) ** 3, nproj, LANES), f32),
            pltpu.VMEM((node_steps, node_buffer, LANES), bf16),
            pltpu.VMEM((node_steps, node_buffer, LANES), bf16),
            pltpu.VMEM((vert_steps, vert_buffer, LANES), bf16),
            pltpu.VMEM((vert_steps, vert_buffer, LANES), bf16),
            pltpu.SemaphoreType.DMA((node_steps, 7)),
            pltpu.SemaphoreType.DMA((node_steps, 7)),
            pltpu.SemaphoreType.DMA((vert_steps, 7)),
            pltpu.SemaphoreType.DMA((vert_steps, 7)),
            pltpu.SemaphoreType.DMA((1,)),
            pltpu.VMEM((nodes, cells, nodes), bf16),
            pltpu.VMEM((padded // LANES, 16 * cells, LANES), f32),
            pltpu.VMEM((cells, padded, corner_span), bf16),
            pltpu.VMEM((block**3, LANES), bf16),
            pltpu.VMEM((3 * block**2, LANES), bf16),
            pltpu.VMEM((groups, slot_rows, LANES), bf16),
            pltpu.VMEM((slot_rows, groups * LANES), bf16),
            pltpu.VMEM((groups, groups * LANES, LANES), bf16),
            pltpu.VMEM((groups - 1, groups * LANES, LANES), bf16),
            pltpu.VMEM((blocks, share_of, LANES), sum_type),
            pltpu.VMEM((blocks - 1, share_of, LANES), sum_type),
            pltpu.SemaphoreType.DMA((3, groups - 1)),
            pltpu.SemaphoreType.DMA((3, groups - 1)),
            pltpu.SemaphoreType.DMA((2,)),
            pltpu.SemaphoreType.DMA((blocks - 1,)),
            pltpu.SemaphoreType.DMA((blocks - 1,)),
        ],
        compiler_params=pltpu.CompilerParams(
            collective_id=0, has_side_effects=True, vmem_limit_bytes=58 * 1024 * 1024
        ),
        cost_estimate=pl.CostEstimate(
            flops=flops, bytes_accessed=cells * nodes * nodes * 2, transcendentals=0
        ),
    )(psi, jnp.transpose(cell_ham, (1, 0, 2)), proj_table, coupling, kinds)


def local(psi, cell_ham, proj_table, coupling, atom_kind):
    return run_filter(psi, cell_ham, proj_table, coupling, atom_kind.reshape(-1))


def solution(mesh):
    in_specs = (
        P("cells", None, None, "bands"),
        P("cells", None, None),
        P(),
        P(),
        P("cells", None, None),
    )
    out_specs = (P("cells", None, None, "bands"), P("cells", "bands"))
    return jax.shard_map(local, mesh=mesh, in_specs=in_specs, out_specs=out_specs, check_vma=False)
```

```python
import functools
import jax
import jax.numpy as jnp
from jax import lax
from jax.experimental import pallas as pl
from jax.experimental.pallas import tpu as pltpu
from jax.sharding import PartitionSpec as P

ORDER = 8
CPD = 2
DEGREE = 3
LANES = 128
f32 = jnp.float32
bf16 = jnp.bfloat16

MESSAGES = [(1, 0, 0), (0, 1, 0), (0, 0, 1), (1, 1, 0), (1, 0, 1), (0, 1, 1), (1, 1, 1)]


def cube_root(amount):
    result = 1
    while (result + 1) ** 3 <= amount:
        result = result + 1
    return result


def message_rows(extent, unit):
    starts, start = [], 0
    for m in MESSAGES:
        free = 3 - sum(m)
        rows = max(extent**free * unit, 16)
        starts.append((start, rows))
        start += rows
    return starts, start


def filter_kernel(
    blocks, groups, side, nodes, psi_ref, ham_hbm, table_ref, coupling_ref, kind_ref, out_ref, corr_ref,
    ham, ya, yb, total, vcell, vb, proj, parts, loc, coef, wgt,
    node_out, node_in, vert_out, vert_in,
    node_ssem, node_rsem, vert_ssem, vert_rsem, ham_sem,
    raw, stage, projt, inner, faces, slots, wide, gram_out, gram_in, summed, summed_in,
    band_ssem, band_rsem, own_sem, cell_ssem, cell_rsem,
):
    block = psi_ref.shape[0]
    edge = block + 1
    pitch = 24
    cells = CPD**3
    cell_edge = ORDER + 1
    kinds = table_ref.shape[0]
    nproj = table_ref.shape[2]
    corners = 8
    corner_span = corners * nproj
    vside = CPD + 1
    me = lax.axis_index("cells")
    offsets = [i * 1 + j * side + k * side * side for i, j, k in MESSAGES]
    ups = [lax.rem(me + o, blocks) for o in offsets]
    downs = [lax.rem(me + blocks - o, blocks) for o in offsets]
    node_rows, _ = message_rows(block, 1)
    vert_rows, _ = message_rows(CPD, nproj)

    ham_copy = pltpu.make_async_copy(ham_hbm, raw, ham_sem.at[0])
    ham_copy.start()

    barrier = pltpu.get_barrier_semaphore()
    group = lax.axis_index("bands")
    cell_peers = [lax.rem(me + j, blocks) for j in range(1, blocks)]
    band_peers = [lax.rem(group + j, groups) for j in range(1, groups)]
    for target in cell_peers:
        pl.semaphore_signal(
            barrier, inc=1, device_id={"cells": target}, device_id_type=pl.DeviceIdType.MESH
        )
    for target in band_peers:
        pl.semaphore_signal(
            barrier, inc=1, device_id={"bands": target}, device_id_type=pl.DeviceIdType.MESH
        )
    pl.semaphore_wait(barrier, len(cell_peers) + len(band_peers))

    pending = []

    def send(out, arrive, ssem, rsem, ranges, step, targets, chosen=range(7)):
        copies = []
        for m in chosen:
            start, rows = ranges[m]
            copy = pltpu.make_async_remote_copy(
                src_ref=out.at[step, pl.ds(start, rows)],
                dst_ref=arrive.at[step, pl.ds(start, rows)],
                send_sem=ssem.at[step, m],
                recv_sem=rsem.at[step, m],
                device_id={"cells": targets[m]},
                device_id_type=pl.DeviceIdType.MESH,
            )
            copy.start()
            copies.append(copy)
        pending.extend(copies)
        return copies

    send_nodes = functools.partial(send, node_out, node_in, node_ssem, node_rsem, node_rows)
    send_verts = functools.partial(send, vert_out, vert_in, vert_ssem, vert_rsem, vert_rows)

    def line(x, y):
        return pl.multiple_of((x * edge + y) * pitch, 8)

    def pack_nodes(field, plane, step, part):
        (s0, _), (s1, _), (s2, _), (s3, _), (s4, _), (s5, _), (s6, _) = node_rows

        def put(start, value):
            node_out[step, pl.ds(start, block), :] = value.astype(bf16)

        def body(x, carry):
            at = pl.multiple_of(x * block, 16)
            if part == 0:
                put(s0 + at, field[pl.ds(line(plane, x), block), :])
            elif part == 1:
                put(s1 + at, field[pl.ds(line(x, plane), block), :])
            else:
                put(s2 + at, field[pl.ds(line(x, 0) + plane, block, pitch), :])
            return carry

        lax.fori_loop(0, block, body, 0, unroll=4)
        if part == 1:
            put(s3, field[pl.ds(((plane * edge) + plane) * pitch, block), :])
        elif part == 2:
            put(s4, field[pl.ds((plane * edge) * pitch + plane, block, pitch), :])
            put(s5, field[pl.ds(plane * pitch + plane, block, pitch * edge), :])
            corner = field[pl.ds((plane * edge + plane) * pitch + plane, 1), :]
            put(s6, jnp.broadcast_to(corner, (block, LANES)))

    def ship_nodes(field, plane, step, targets, parts=(2, 1, 0)):
        copies = []
        for part in parts:
            pack_nodes(field, plane, step, part)
            chosen = [m for m in range(7) if max(d for d in range(3) if MESSAGES[m][d]) == part]
            copies += send_nodes(step, targets, chosen)
        return copies

    def unpack_nodes(field, plane, step, add):
        (s0, _), (s1, _), (s2, _), (s3, _), (s4, _), (s5, _), (s6, _) = node_rows

        def put(where, start):
            value = node_in[step, pl.ds(start, block), :].astype(f32)
            if add:
                value = field[where, :] + value
            field[where, :] = value

        def body(x, carry):
            at = pl.multiple_of(x * block, 16)
            put(pl.ds(line(plane, x), block), s0 + at)
            put(pl.ds(line(x, plane), block), s1 + at)
            put(pl.ds(line(x, 0) + plane, block, pitch), s2 + at)
            return carry

        lax.fori_loop(0, block, body, 0)
        put(pl.ds(((plane * edge) + plane) * pitch, block), s3)
        put(pl.ds((plane * edge) * pitch + plane, block, pitch), s4)
        put(pl.ds(plane * pitch + plane, block, pitch * edge), s5)
        where = pl.ds((plane * edge + plane) * pitch + plane, 1)
        value = node_in[step, pl.ds(s6, block), :].astype(f32)[0:1]
        if add:
            value = field[where, :] + value
        field[where, :] = value

    def vertex_places(plane):
        places = []
        for m, (start, _) in zip(MESSAGES, vert_rows):
            spans = [[plane] if fixed else list(range(CPD)) for fixed in m]
            at = start
            for i in spans[0]:
                for j in spans[1]:
                    for k in spans[2]:
                        places.append(((i * vside + j) * vside + k, at))
                        at += nproj
        return places

    def pack_verts(field, plane, step):
        for vertex, at in vertex_places(plane):
            vert_out[step, pl.ds(at, nproj), :] = field[vertex].astype(bf16)

    def unpack_verts(field, plane, step, add):
        for vertex, at in vertex_places(plane):
            value = vert_in[step, pl.ds(at, nproj), :].astype(f32)
            field[vertex] = field[vertex] + value if add else value

    def arrived(copies):
        for copy in copies:
            copy.wait_recv()

    owned = [
        ((i * vside + j) * vside + k, (i * CPD + j) * CPD + k)
        for i in range(CPD) for j in range(CPD) for k in range(CPD)
    ]

    def load_psi(x, carry):
        for y in range(block):
            value = psi_ref[x, y].astype(f32)
            ya[pl.ds(line(x, y), block), :] = value
        return carry

    lax.fori_loop(0, block, load_psi, 0)
    psi_copies = ship_nodes(ya, 0, 0, downs)
    for vertex, position in owned:
        wgt[vertex] = jnp.full((nproj, LANES), kind_ref[position // 4, (position // 2) % 2, position % 2].astype(f32), f32)
    pack_verts(wgt, 0, 0)
    kind_copies = send_verts(0, downs)

    full, tail = nodes // 16, nodes % 16
    chunks = [(n, start, min(LANES, nodes - start)) for n, start in enumerate(range(0, nodes, LANES))]

    def relayout(t, rows):
        for r in range(rows):
            value = raw[t * 16 + r].astype(f32)
            for n, start, width in chunks:
                stage[n, r * cells : (r + 1) * cells, 0:width] = value[:, start : start + width]
        for c in range(cells):
            for n, start, _ in chunks:
                value = stage[n, pl.ds(c, 16, cells), :].astype(bf16)
                ham[c, pl.ds(pl.multiple_of(t * 16, 16), 16), start : start + LANES] = value

    def relayout_body(t, carry):
        relayout(t, 16)
        return carry

    early = full * 2 // 3
    stage[...] = jnp.zeros_like(stage)
    ham_copy.wait()
    lax.fori_loop(0, early, relayout_body, 0)
    proj[...] = jnp.zeros_like(proj)
    vcell[...] = jnp.zeros_like(vcell)
    arrived(kind_copies)
    unpack_verts(wgt, CPD, 0, False)

    def place(c):
        ca = c // (CPD * CPD)
        cb = lax.rem(c // CPD, CPD)
        cc = lax.rem(c, CPD)
        return ca, cb, cc

    def corner_vertex(c, o):
        ca, cb, cc = place(c)
        return ((ca + o // 4) * vside + cb + (o // 2) % 2) * vside + cc + o % 2

    def select(c, carry):
        for o in range(corners):
            mark = wgt[corner_vertex(c, o)]
            start = 0
            while start < nodes:
                width = min(LANES, nodes - start)
                chosen = jnp.zeros((nproj, width), f32)
                for q in range(kinds):
                    row = table_ref[q, o, :, start : start + width].astype(f32)
                    chosen = jnp.where(mark[:, :width] == float(q), row, chosen)
                proj[c, o * nproj : (o + 1) * nproj, start : start + width] = chosen.astype(bf16)
                start += LANES
        projt[c] = jnp.transpose(proj[c].astype(f32)).astype(bf16)
        return carry

    lax.fori_loop(0, cells, select, 0)
    arrived(psi_copies)
    unpack_nodes(ya, block, 0, False)

    def cell_base(c):
        ca, cb, cc = place(c)
        return ((ca * ORDER) * edge + cb * ORDER) * pitch + cc * ORDER

    depth = lax.broadcasted_iota(jnp.int32, (block, LANES), 0)
    share_rows = block**3 // groups
    face_rows = 3 * block * block // groups

    def share(source, start, rows, kind):
        copies = []
        for j, target in enumerate(band_peers):
            copies.append(
                pltpu.make_async_remote_copy(
                    src_ref=source.at[pl.ds(pl.multiple_of(target * rows, 16), rows)],
                    dst_ref=slots.at[group, pl.ds(start, rows)],
                    send_sem=band_ssem.at[kind, j],
                    recv_sem=band_rsem.at[kind, j],
                    device_id={"bands": target},
                    device_id_type=pl.DeviceIdType.MESH,
                )
            )
            copies[-1].start()
        pending.extend(copies)
        own = pltpu.make_async_copy(
            source.at[pl.ds(pl.multiple_of(group * rows, 16), rows)],
            slots.at[group, pl.ds(start, rows)],
            own_sem.at[kind],
        )
        own.start()
        return copies, own

    current, previous = ya, yb
    node_step, vert_step = 1, 1
    for degree in range(DEGREE):

        def gather(c, carry):
            base = cell_base(c)
            for x in range(cell_edge):
                for y in range(cell_edge):
                    at = pl.multiple_of(base + (x * edge + y) * pitch, 8)
                    row = (x * cell_edge + y) * cell_edge
                    vcell[row : row + 8, :] = current[pl.ds(at, 8), :]
                    vcell[row + 8 : row + 9, :] = current[pl.ds(at + 8, 1), :]
            values = vcell[...].astype(bf16)
            vb[c] = values
            parts[c] = jnp.dot(proj[c], values, preferred_element_type=f32)
            return carry

        lax.fori_loop(0, cells, gather, 0, unroll=2)
        coef[...] = jnp.zeros_like(coef)
        for c in range(cells):
            ca, cb, cc = c // 4, (c // 2) % 2, c % 2
            for o in range(corners):
                vertex = ((ca + o // 4) * vside + cb + (o // 2) % 2) * vside + cc + o % 2
                coef[vertex] = coef[vertex] + parts[c, o * nproj : (o + 1) * nproj, :]
        pack_verts(coef, CPD, vert_step)
        coef_copies = send_verts(vert_step, ups)

        if degree == 0:
            lax.fori_loop(early, full, relayout_body, 0)
            if tail:
                stage[:, tail * cells :, :] = jnp.zeros((len(chunks), (16 - tail) * cells, LANES), f32)
                relayout(full, tail)

        def multiply(c, carry):
            loc[c, 0 : ham.shape[1], :] = jnp.dot(ham[c], vb[c], preferred_element_type=f32)
            return carry

        half = cells // 2
        lax.fori_loop(0, half, multiply, 0)
        arrived(coef_copies)
        unpack_verts(coef, 0, vert_step, True)
        for vertex, position in owned:
            kind = kind_ref[position // 4, (position // 2) % 2, position % 2]
            matrix = coupling_ref[jnp.maximum(kind, 0)]
            matrix = jnp.where(kind >= 0, matrix, 0.0)
            value = jnp.dot(
                matrix, coef[vertex], precision=lax.Precision.HIGHEST, preferred_element_type=f32
            )
            wgt[vertex] = value.astype(bf16).astype(f32)
        pack_verts(wgt, 0, vert_step + 1)
        weight_copies = send_verts(vert_step + 1, downs)
        lax.fori_loop(half, cells, multiply, 0)
        total[...] = jnp.zeros_like(total)
        arrived(weight_copies)
        unpack_verts(wgt, CPD, vert_step + 1, False)
        vert_step += 2

        def scatter(c, carry):
            weights = jnp.concatenate([wgt[corner_vertex(c, o)] for o in range(corners)], axis=0)
            vcell[...] = jnp.dot(projt[c], weights.astype(bf16), preferred_element_type=f32)
            base = cell_base(c)
            for x in range(cell_edge):
                stores = []
                for y in range(cell_edge):
                    at = pl.multiple_of(base + (x * edge + y) * pitch, 8)
                    row = (x * cell_edge + y) * cell_edge
                    for place_in, rows, size in ((at, row, 8), (at + 8, row + 8, 1)):
                        where = pl.ds(place_in, size)
                        value = vcell[rows : rows + size, :] + loc[c, rows : rows + size, :]
                        stores.append((where, total[where, :] + value))
                for where, value in stores:
                    total[where, :] = value
            return carry

        fold_copies = []
        for part, stride in ((2, 2), (1, CPD * CPD), (0, CPD * CPD)):
            start = (0, 2, 1)[part]
            lax.fori_loop(
                0, cells // stride, lambda t, carry: scatter(t * stride + start, carry), 0
            )
            fold_copies += ship_nodes(total, block, node_step, ups, (part,))
        first, last = degree == 0, degree == DEGREE - 1

        def advanced(x, y):
            where = pl.ds(line(x, y), block)
            value = total[where, :] - current[where, :]
            if not first:
                value = 2.0 * value - previous[where, :]
            return value.astype(bf16)

        if last:
            def interior(x, carry):
                keep = (depth > 0) & (x > 0)
                for y in range(1, block):
                    value = jnp.where(keep, advanced(x, y).astype(f32), 0.0)
                    inner[pl.ds(pl.multiple_of((x * block + y) * block, 16), block), :] = value.astype(bf16)
                inner[pl.ds(pl.multiple_of(x * block * block, 16), block), :] = jnp.zeros((block, LANES), bf16)
                return carry

            lax.fori_loop(0, block, interior, 0)
            inner_copies = share(inner, 0, share_rows, 0)
        arrived(fold_copies)
        unpack_nodes(total, 0, node_step, True)
        node_step += 1

        def update(x, carry):
            for start in range(0, block, 4):
                stores = [(y, advanced(x, y)) for y in range(start, start + 4)]
                for y, value in stores:
                    if last:
                        out_ref[x, y] = value
                    previous[pl.ds(line(x, y), block), :] = value.astype(f32)
            return carry

        lax.fori_loop(0, block, update, 0)
        if not last:
            field_copies = ship_nodes(previous, 0, node_step, downs)
            arrived(field_copies)
            unpack_nodes(previous, block, node_step, False)
            node_step += 1
        current, previous = previous, current

    lines = block // groups

    def pack_faces(x, carry):
        at = (x // lines) * face_rows + lax.rem(x, lines) * block
        rows = lines * block
        low = current[pl.ds(line(x, 0), block, pitch), :]
        side_face = jnp.where(depth > 0, current[pl.ds(line(x, 0), block), :], 0.0)
        front = jnp.where((depth > 0) & (x > 0), current[pl.ds(line(0, x), block), :], 0.0)
        for part, value in enumerate((low, side_face, front)):
            faces[pl.ds(pl.multiple_of(at + part * rows, 16), block), :] = value.astype(bf16)
        return carry

    lax.fori_loop(0, block, pack_faces, 0)
    face_copies = share(faces, share_rows, face_rows, 1)
    for copies, own in (inner_copies, face_copies):
        own.wait()
        arrived(copies)
    for g in range(groups):
        wide[:, g * LANES : (g + 1) * LANES] = slots[g]
    for g in range(groups):
        product = lax.dot_general(
            wide[:, g * LANES : (g + 1) * LANES], wide[...],
            (((0,), (0,)), ((), ())), preferred_element_type=f32,
        )
        for h in range(groups):
            gram_out[h, g * LANES : (g + 1) * LANES, :] = product[:, h * LANES : (h + 1) * LANES].astype(bf16)
    gram_copies = []
    for j, target in enumerate(band_peers):
        copy = pltpu.make_async_remote_copy(
            src_ref=gram_out.at[target],
            dst_ref=gram_in.at[j],
            send_sem=band_ssem.at[2, j],
            recv_sem=band_rsem.at[2, j],
            device_id={"bands": target},
            device_id_type=pl.DeviceIdType.MESH,
        )
        copy.start()
        gram_copies.append(copy)
    pending.extend(gram_copies)
    arrived(gram_copies)
    share_of = summed.shape[1]
    scale = 1.0 / (blocks * block**3)
    tile = max(share_of, 16)
    for start in range(0, groups * LANES, tile):
        value = gram_out[group, start : start + tile, :].astype(f32)
        for j in range(groups - 1):
            value = value + gram_in[j, start : start + tile, :].astype(f32)
        value = value * scale
        for row in range(0, tile, share_of):
            summed[(start + row) // share_of] = value[row : row + share_of].astype(summed.dtype)
    sum_copies = []
    for j, target in enumerate(cell_peers):
        copy = pltpu.make_async_remote_copy(
            src_ref=summed.at[target],
            dst_ref=summed_in.at[j],
            send_sem=cell_ssem.at[j],
            recv_sem=cell_rsem.at[j],
            device_id={"cells": target},
            device_id_type=pl.DeviceIdType.MESH,
        )
        copy.start()
        sum_copies.append(copy)
    pending.extend(sum_copies)
    value = summed[me].astype(f32)
    for j, copy in enumerate(sum_copies):
        copy.wait_recv()
        value = value + summed_in[j].astype(f32)
    corr_ref[...] = value

    for copy in pending:
        copy.wait_send()


def run_filter(psi, cell_ham, proj_table, coupling, kinds):
    blocks = lax.axis_size("cells")
    groups = lax.axis_size("bands")
    side = cube_root(blocks)
    share_of = groups * LANES // blocks
    sum_type = f32 if share_of % 16 else bf16
    slot_rows = (psi.shape[0] ** 3 + 3 * psi.shape[0] ** 2) // groups
    block = psi.shape[0]
    nodes = cell_ham.shape[-1]
    cells = cell_ham.shape[0]
    padded = -(-nodes // LANES) * LANES
    nproj = proj_table.shape[2]
    corner_span = 8 * nproj
    rows = (block + 1) ** 2 * 24
    node_steps, vert_steps = 2 * DEGREE, 2 * DEGREE + 1
    _, node_buffer = message_rows(block, 1)
    _, vert_buffer = message_rows(CPD, nproj)
    vmem = pl.BlockSpec(memory_space=pltpu.VMEM)
    flops = DEGREE * cells * 2 * LANES * nodes * (nodes + 2 * corner_span)
    return pl.pallas_call(
        functools.partial(filter_kernel, blocks, groups, side, nodes),
        out_shape=(
            jax.ShapeDtypeStruct(psi.shape, bf16),
            jax.ShapeDtypeStruct((share_of, LANES), f32),
        ),
        in_specs=[
            vmem,
            pl.BlockSpec(memory_space=pl.ANY),
            vmem,
            vmem,
            pl.BlockSpec(memory_space=pltpu.SMEM),
        ],
        out_specs=(vmem, vmem),
        scratch_shapes=[
            pltpu.VMEM((cells, -(-nodes // 16) * 16, padded), bf16),
            pltpu.VMEM((rows, LANES), f32),
            pltpu.VMEM((rows, LANES), f32),
            pltpu.VMEM((rows, LANES), f32),
            pltpu.VMEM((padded, LANES), f32),
            pltpu.VMEM((cells, padded, LANES), bf16),
            pltpu.VMEM((cells, corner_span, padded), bf16),
            pltpu.VMEM((cells, corner_span, LANES), f32),
            pltpu.VMEM((cells, padded, LANES), f32),
            pltpu.VMEM(((CPD + 1) ** 3, nproj, LANES), f32),
            pltpu.VMEM(((CPD + 1) ** 3, nproj, LANES), f32),
            pltpu.VMEM((node_steps, node_buffer, LANES), bf16),
            pltpu.VMEM((node_steps, node_buffer, LANES), bf16),
            pltpu.VMEM((vert_steps, vert_buffer, LANES), bf16),
            pltpu.VMEM((vert_steps, vert_buffer, LANES), bf16),
            pltpu.SemaphoreType.DMA((node_steps, 7)),
            pltpu.SemaphoreType.DMA((node_steps, 7)),
            pltpu.SemaphoreType.DMA((vert_steps, 7)),
            pltpu.SemaphoreType.DMA((vert_steps, 7)),
            pltpu.SemaphoreType.DMA((1,)),
            pltpu.VMEM((nodes, cells, nodes), bf16),
            pltpu.VMEM((padded // LANES, 16 * cells, LANES), f32),
            pltpu.VMEM((cells, padded, corner_span), bf16),
            pltpu.VMEM((block**3, LANES), bf16),
            pltpu.VMEM((3 * block**2, LANES), bf16),
            pltpu.VMEM((groups, slot_rows, LANES), bf16),
            pltpu.VMEM((slot_rows, groups * LANES), bf16),
            pltpu.VMEM((groups, groups * LANES, LANES), bf16),
            pltpu.VMEM((groups - 1, groups * LANES, LANES), bf16),
            pltpu.VMEM((blocks, share_of, LANES), sum_type),
            pltpu.VMEM((blocks - 1, share_of, LANES), sum_type),
            pltpu.SemaphoreType.DMA((3, groups - 1)),
            pltpu.SemaphoreType.DMA((3, groups - 1)),
            pltpu.SemaphoreType.DMA((2,)),
            pltpu.SemaphoreType.DMA((blocks - 1,)),
            pltpu.SemaphoreType.DMA((blocks - 1,)),
        ],
        compiler_params=pltpu.CompilerParams(
            collective_id=0, has_side_effects=True, vmem_limit_bytes=50 * 1024 * 1024
        ),
        cost_estimate=pl.CostEstimate(
            flops=flops, bytes_accessed=cells * nodes * nodes * 2, transcendentals=0
        ),
    )(psi, jnp.transpose(cell_ham, (1, 0, 2)), proj_table, coupling, kinds)


def local(psi, cell_ham, proj_table, coupling, atom_kind):
    return run_filter(psi, cell_ham, proj_table, coupling, atom_kind)


def solution(mesh):
    in_specs = (
        P("cells", None, None, "bands"),
        P("cells", None, None),
        P(),
        P(),
        P("cells", None, None),
    )
    out_specs = (P("cells", None, None, "bands"), P("cells", "bands"))
    return jax.shard_map(local, mesh=mesh, in_specs=in_specs, out_specs=out_specs, check_vma=False)
```

```python
import functools
import jax
import jax.numpy as jnp
from jax import lax
from jax.experimental import pallas as pl
from jax.experimental.pallas import tpu as pltpu
from jax.sharding import PartitionSpec as P

ORDER = 8
CPD = 2
DEGREE = 3
LANES = 128
f32 = jnp.float32
bf16 = jnp.bfloat16

MESSAGES = [(1, 0, 0), (0, 1, 0), (0, 0, 1), (1, 1, 0), (1, 0, 1), (0, 1, 1), (1, 1, 1)]


def cube_root(amount):
    result = 1
    while (result + 1) ** 3 <= amount:
        result = result + 1
    return result


def message_rows(extent, unit):
    starts, start = [], 0
    for m in MESSAGES:
        free = 3 - sum(m)
        rows = max(extent**free * unit, 16)
        starts.append((start, rows))
        start += rows
    return starts, start


def filter_kernel(
    blocks, groups, side, nodes, psi_ref, ham_hbm, table_ref, coupling_ref, kind_ref, out_ref, corr_ref,
    ham, ya, yb, total, vcell, vb, proj, parts, loc, coef, wgt,
    node_out, node_in, vert_out, vert_in,
    node_ssem, node_rsem, vert_ssem, vert_rsem, ham_sem,
    raw, stage, projt, inner, faces, slots, wide, gram_out, gram_in, summed, summed_in,
    band_ssem, band_rsem, own_sem, cell_ssem, cell_rsem,
):
    block = psi_ref.shape[0]
    edge = block + 1
    pitch = 24
    cells = CPD**3
    cell_edge = ORDER + 1
    kinds = table_ref.shape[0]
    nproj = table_ref.shape[2]
    corners = 8
    corner_span = corners * nproj
    vside = CPD + 1
    me = lax.axis_index("cells")
    offsets = [i * 1 + j * side + k * side * side for i, j, k in MESSAGES]
    ups = [lax.rem(me + o, blocks) for o in offsets]
    downs = [lax.rem(me + blocks - o, blocks) for o in offsets]
    node_rows, _ = message_rows(block, 1)
    vert_rows, _ = message_rows(CPD, nproj)

    ham_copy = pltpu.make_async_copy(ham_hbm, raw, ham_sem.at[0])
    ham_copy.start()

    barrier = pltpu.get_barrier_semaphore()
    group = lax.axis_index("bands")
    cell_peers = [lax.rem(me + j, blocks) for j in range(1, blocks)]
    band_peers = [lax.rem(group + j, groups) for j in range(1, groups)]
    for target in cell_peers:
        pl.semaphore_signal(
            barrier, inc=1, device_id={"cells": target}, device_id_type=pl.DeviceIdType.MESH
        )
    for target in band_peers:
        pl.semaphore_signal(
            barrier, inc=1, device_id={"bands": target}, device_id_type=pl.DeviceIdType.MESH
        )
    pl.semaphore_wait(barrier, len(cell_peers) + len(band_peers))

    pending = []

    def send(out, arrive, ssem, rsem, ranges, step, targets, chosen=range(7)):
        copies = []
        for m in chosen:
            start, rows = ranges[m]
            copy = pltpu.make_async_remote_copy(
                src_ref=out.at[step, pl.ds(start, rows)],
                dst_ref=arrive.at[step, pl.ds(start, rows)],
                send_sem=ssem.at[step, m],
                recv_sem=rsem.at[step, m],
                device_id={"cells": targets[m]},
                device_id_type=pl.DeviceIdType.MESH,
            )
            copy.start()
            copies.append(copy)
        pending.extend(copies)
        return copies

    send_nodes = functools.partial(send, node_out, node_in, node_ssem, node_rsem, node_rows)
    send_verts = functools.partial(send, vert_out, vert_in, vert_ssem, vert_rsem, vert_rows)

    def line(x, y):
        return pl.multiple_of((x * edge + y) * pitch, 8)

    def pack_nodes(field, plane, step, part):
        (s0, _), (s1, _), (s2, _), (s3, _), (s4, _), (s5, _), (s6, _) = node_rows

        def put(start, value):
            node_out[step, pl.ds(start, block), :] = value.astype(bf16)

        def body(x, carry):
            at = pl.multiple_of(x * block, 16)
            if part == 0:
                put(s0 + at, field[pl.ds(line(plane, x), block), :])
            elif part == 1:
                put(s1 + at, field[pl.ds(line(x, plane), block), :])
            else:
                put(s2 + at, field[pl.ds(line(x, 0) + plane, block, pitch), :])
            return carry

        lax.fori_loop(0, block, body, 0, unroll=4)
        if part == 1:
            put(s3, field[pl.ds(((plane * edge) + plane) * pitch, block), :])
        elif part == 2:
            put(s4, field[pl.ds((plane * edge) * pitch + plane, block, pitch), :])
            put(s5, field[pl.ds(plane * pitch + plane, block, pitch * edge), :])
            corner = field[pl.ds((plane * edge + plane) * pitch + plane, 1), :]
            put(s6, jnp.broadcast_to(corner, (block, LANES)))

    def ship_nodes(field, plane, step, targets, parts=(2, 1, 0)):
        copies = []
        for part in parts:
            pack_nodes(field, plane, step, part)
            chosen = [m for m in range(7) if max(d for d in range(3) if MESSAGES[m][d]) == part]
            copies += send_nodes(step, targets, chosen)
        return copies

    def unpack_nodes(field, plane, step, add):
        (s0, _), (s1, _), (s2, _), (s3, _), (s4, _), (s5, _), (s6, _) = node_rows

        def put(where, start):
            value = node_in[step, pl.ds(start, block), :].astype(f32)
            if add:
                value = field[where, :] + value
            field[where, :] = value

        def body(x, carry):
            at = pl.multiple_of(x * block, 16)
            put(pl.ds(line(plane, x), block), s0 + at)
            put(pl.ds(line(x, plane), block), s1 + at)
            put(pl.ds(line(x, 0) + plane, block, pitch), s2 + at)
            return carry

        lax.fori_loop(0, block, body, 0, unroll=4)
        put(pl.ds(((plane * edge) + plane) * pitch, block), s3)
        put(pl.ds((plane * edge) * pitch + plane, block, pitch), s4)
        put(pl.ds(plane * pitch + plane, block, pitch * edge), s5)
        where = pl.ds((plane * edge + plane) * pitch + plane, 1)
        value = node_in[step, pl.ds(s6, block), :].astype(f32)[0:1]
        if add:
            value = field[where, :] + value
        field[where, :] = value

    def vertex_places(plane):
        places = []
        for m, (start, _) in zip(MESSAGES, vert_rows):
            spans = [[plane] if fixed else list(range(CPD)) for fixed in m]
            at = start
            for i in spans[0]:
                for j in spans[1]:
                    for k in spans[2]:
                        places.append(((i * vside + j) * vside + k, at))
                        at += nproj
        return places

    def pack_verts(field, plane, step):
        for vertex, at in vertex_places(plane):
            vert_out[step, pl.ds(at, nproj), :] = field[vertex].astype(bf16)

    def unpack_verts(field, plane, step, add):
        for vertex, at in vertex_places(plane):
            value = vert_in[step, pl.ds(at, nproj), :].astype(f32)
            field[vertex] = field[vertex] + value if add else value

    def arrived(copies):
        for copy in copies:
            copy.wait_recv()

    owned = [
        ((i * vside + j) * vside + k, (i * CPD + j) * CPD + k)
        for i in range(CPD) for j in range(CPD) for k in range(CPD)
    ]

    def load_psi(x, carry):
        for y in range(block):
            value = psi_ref[x, y].astype(f32)
            ya[pl.ds(line(x, y), block), :] = value
        return carry

    lax.fori_loop(0, block, load_psi, 0)
    psi_copies = ship_nodes(ya, 0, 0, downs)
    for vertex, position in owned:
        wgt[vertex] = jnp.full((nproj, LANES), kind_ref[position // 4, (position // 2) % 2, position % 2].astype(f32), f32)
    pack_verts(wgt, 0, 0)
    kind_copies = send_verts(0, downs)

    full, tail = nodes // 16, nodes % 16
    chunks = [(n, start, min(LANES, nodes - start)) for n, start in enumerate(range(0, nodes, LANES))]

    def relayout(t, rows):
        for r in range(rows):
            value = raw[t * 16 + r].astype(f32)
            for n, start, width in chunks:
                stage[n, r * cells : (r + 1) * cells, 0:width] = value[:, start : start + width]
        for c in range(cells):
            for n, start, _ in chunks:
                value = stage[n, pl.ds(c, 16, cells), :].astype(bf16)
                ham[c, pl.ds(pl.multiple_of(t * 16, 16), 16), start : start + LANES] = value

    def relayout_body(t, carry):
        relayout(t, 16)
        return carry

    early = full * 2 // 3
    stage[...] = jnp.zeros_like(stage)
    ham_copy.wait()
    lax.fori_loop(0, early, relayout_body, 0)
    proj[...] = jnp.zeros_like(proj)
    vcell[...] = jnp.zeros_like(vcell)
    arrived(kind_copies)
    unpack_verts(wgt, CPD, 0, False)

    def place(c):
        ca = c // (CPD * CPD)
        cb = lax.rem(c // CPD, CPD)
        cc = lax.rem(c, CPD)
        return ca, cb, cc

    def corner_vertex(c, o):
        ca, cb, cc = place(c)
        return ((ca + o // 4) * vside + cb + (o // 2) % 2) * vside + cc + o % 2

    def select(c, carry):
        for o in range(corners):
            mark = wgt[corner_vertex(c, o)]
            start = 0
            while start < nodes:
                width = min(LANES, nodes - start)
                chosen = jnp.zeros((nproj, width), f32)
                for q in range(kinds):
                    row = table_ref[q, o, :, start : start + width].astype(f32)
                    chosen = jnp.where(mark[:, :width] == float(q), row, chosen)
                proj[c, o * nproj : (o + 1) * nproj, start : start + width] = chosen.astype(bf16)
                start += LANES
        projt[c] = jnp.transpose(proj[c].astype(f32)).astype(bf16)
        return carry

    lax.fori_loop(0, cells, select, 0)
    arrived(psi_copies)
    unpack_nodes(ya, block, 0, False)

    def cell_base(c):
        ca, cb, cc = place(c)
        return ((ca * ORDER) * edge + cb * ORDER) * pitch + cc * ORDER

    depth = lax.broadcasted_iota(jnp.int32, (block, LANES), 0)
    share_rows = block**3 // groups
    face_rows = 3 * block * block // groups

    def share(source, start, rows, kind):
        copies = []
        for j, target in enumerate(band_peers):
            copies.append(
                pltpu.make_async_remote_copy(
                    src_ref=source.at[pl.ds(pl.multiple_of(target * rows, 16), rows)],
                    dst_ref=slots.at[group, pl.ds(start, rows)],
                    send_sem=band_ssem.at[kind, j],
                    recv_sem=band_rsem.at[kind, j],
                    device_id={"bands": target},
                    device_id_type=pl.DeviceIdType.MESH,
                )
            )
            copies[-1].start()
        pending.extend(copies)
        own = pltpu.make_async_copy(
            source.at[pl.ds(pl.multiple_of(group * rows, 16), rows)],
            slots.at[group, pl.ds(start, rows)],
            own_sem.at[kind],
        )
        own.start()
        return copies, own

    current, previous = ya, yb
    node_step, vert_step = 1, 1
    for degree in range(DEGREE):

        def gather(c, carry):
            base = cell_base(c)
            for x in range(cell_edge):
                for y in range(cell_edge):
                    at = pl.multiple_of(base + (x * edge + y) * pitch, 8)
                    row = (x * cell_edge + y) * cell_edge
                    vcell[row : row + 8, :] = current[pl.ds(at, 8), :]
                    vcell[row + 8 : row + 9, :] = current[pl.ds(at + 8, 1), :]
            values = vcell[...].astype(bf16)
            vb[c] = values
            parts[c] = jnp.dot(proj[c], values, preferred_element_type=f32)
            return carry

        lax.fori_loop(0, cells, gather, 0, unroll=2)
        coef[...] = jnp.zeros_like(coef)
        for c in range(cells):
            ca, cb, cc = c // 4, (c // 2) % 2, c % 2
            for o in range(corners):
                vertex = ((ca + o // 4) * vside + cb + (o // 2) % 2) * vside + cc + o % 2
                coef[vertex] = coef[vertex] + parts[c, o * nproj : (o + 1) * nproj, :]
        pack_verts(coef, CPD, vert_step)
        coef_copies = send_verts(vert_step, ups)

        if degree == 0:
            lax.fori_loop(early, full, relayout_body, 0)
            if tail:
                stage[:, tail * cells :, :] = jnp.zeros((len(chunks), (16 - tail) * cells, LANES), f32)
                relayout(full, tail)

        def multiply(c, carry):
            loc[c, 0 : ham.shape[1], :] = jnp.dot(ham[c], vb[c], preferred_element_type=f32)
            return carry

        half = cells // 2
        lax.fori_loop(0, half, multiply, 0, unroll=2)
        arrived(coef_copies)
        unpack_verts(coef, 0, vert_step, True)
        for vertex, position in owned:
            kind = kind_ref[position // 4, (position // 2) % 2, position % 2]
            matrix = coupling_ref[jnp.maximum(kind, 0)]
            matrix = jnp.where(kind >= 0, matrix, 0.0)
            value = jnp.dot(
                matrix, coef[vertex], precision=lax.Precision.HIGHEST, preferred_element_type=f32
            )
            wgt[vertex] = value.astype(bf16).astype(f32)
        pack_verts(wgt, 0, vert_step + 1)
        weight_copies = send_verts(vert_step + 1, downs)
        lax.fori_loop(half, cells, multiply, 0, unroll=2)
        total[...] = jnp.zeros_like(total)
        arrived(weight_copies)
        unpack_verts(wgt, CPD, vert_step + 1, False)
        vert_step += 2

        def scatter(c, carry):
            weights = jnp.concatenate([wgt[corner_vertex(c, o)] for o in range(corners)], axis=0)
            vcell[...] = jnp.dot(projt[c], weights.astype(bf16), preferred_element_type=f32)
            base = cell_base(c)
            for x in range(cell_edge):
                stores = []
                for y in range(cell_edge):
                    at = pl.multiple_of(base + (x * edge + y) * pitch, 8)
                    row = (x * cell_edge + y) * cell_edge
                    for place_in, rows, size in ((at, row, 8), (at + 8, row + 8, 1)):
                        where = pl.ds(place_in, size)
                        value = vcell[rows : rows + size, :] + loc[c, rows : rows + size, :]
                        stores.append((where, total[where, :] + value))
                for where, value in stores:
                    total[where, :] = value
            return carry

        fold_copies = []
        for part, stride in ((2, 2), (1, CPD * CPD), (0, CPD * CPD)):
            start = (0, 2, 1)[part]
            lax.fori_loop(
                0, cells // stride, lambda t, carry: scatter(t * stride + start, carry), 0
            )
            fold_copies += ship_nodes(total, block, node_step, ups, (part,))
        first, last = degree == 0, degree == DEGREE - 1

        def advanced(x, y):
            where = pl.ds(line(x, y), block)
            value = total[where, :] - current[where, :]
            if not first:
                value = 2.0 * value - previous[where, :]
            return value.astype(bf16)

        if last:
            def interior(x, carry):
                keep = (depth > 0) & (x > 0)
                for y in range(1, block):
                    value = jnp.where(keep, advanced(x, y).astype(f32), 0.0)
                    inner[pl.ds(pl.multiple_of((x * block + y) * block, 16), block), :] = value.astype(bf16)
                inner[pl.ds(pl.multiple_of(x * block * block, 16), block), :] = jnp.zeros((block, LANES), bf16)
                return carry

            lax.fori_loop(0, block, interior, 0)
            inner_copies = share(inner, 0, share_rows, 0)
        arrived(fold_copies)
        unpack_nodes(total, 0, node_step, True)
        node_step += 1

        def update(x, carry):
            for start in range(0, block, 4):
                stores = [(y, advanced(x, y)) for y in range(start, start + 4)]
                for y, value in stores:
                    if last:
                        out_ref[x, y] = value
                    previous[pl.ds(line(x, y), block), :] = value.astype(f32)
            return carry

        lax.fori_loop(0, block, update, 0)
        if not last:
            field_copies = ship_nodes(previous, 0, node_step, downs)
            arrived(field_copies)
            unpack_nodes(previous, block, node_step, False)
            node_step += 1
        current, previous = previous, current

    lines = block // groups

    def pack_faces(x, carry):
        at = (x // lines) * face_rows + lax.rem(x, lines) * block
        rows = lines * block
        low = current[pl.ds(line(x, 0), block, pitch), :]
        side_face = jnp.where(depth > 0, current[pl.ds(line(x, 0), block), :], 0.0)
        front = jnp.where((depth > 0) & (x > 0), current[pl.ds(line(0, x), block), :], 0.0)
        for part, value in enumerate((low, side_face, front)):
            faces[pl.ds(pl.multiple_of(at + part * rows, 16), block), :] = value.astype(bf16)
        return carry

    lax.fori_loop(0, block, pack_faces, 0)
    face_copies = share(faces, share_rows, face_rows, 1)
    for copies, own in (inner_copies, face_copies):
        own.wait()
        arrived(copies)
    for g in range(groups):
        wide[:, g * LANES : (g + 1) * LANES] = slots[g]
    for g in range(groups):
        product = lax.dot_general(
            wide[:, g * LANES : (g + 1) * LANES], wide[...],
            (((0,), (0,)), ((), ())), preferred_element_type=f32,
        )
        for h in range(groups):
            gram_out[h, g * LANES : (g + 1) * LANES, :] = product[:, h * LANES : (h + 1) * LANES].astype(bf16)
    gram_copies = []
    for j, target in enumerate(band_peers):
        copy = pltpu.make_async_remote_copy(
            src_ref=gram_out.at[target],
            dst_ref=gram_in.at[j],
            send_sem=band_ssem.at[2, j],
            recv_sem=band_rsem.at[2, j],
            device_id={"bands": target},
            device_id_type=pl.DeviceIdType.MESH,
        )
        copy.start()
        gram_copies.append(copy)
    pending.extend(gram_copies)
    arrived(gram_copies)
    share_of = summed.shape[1]
    scale = 1.0 / (blocks * block**3)
    tile = max(share_of, 16)
    for start in range(0, groups * LANES, tile):
        value = gram_out[group, start : start + tile, :].astype(f32)
        for j in range(groups - 1):
            value = value + gram_in[j, start : start + tile, :].astype(f32)
        value = value * scale
        for row in range(0, tile, share_of):
            summed[(start + row) // share_of] = value[row : row + share_of].astype(summed.dtype)
    sum_copies = []
    for j, target in enumerate(cell_peers):
        copy = pltpu.make_async_remote_copy(
            src_ref=summed.at[target],
            dst_ref=summed_in.at[j],
            send_sem=cell_ssem.at[j],
            recv_sem=cell_rsem.at[j],
            device_id={"cells": target},
            device_id_type=pl.DeviceIdType.MESH,
        )
        copy.start()
        sum_copies.append(copy)
    pending.extend(sum_copies)
    value = summed[me].astype(f32)
    for j, copy in enumerate(sum_copies):
        copy.wait_recv()
        value = value + summed_in[j].astype(f32)
    corr_ref[...] = value

    for copy in pending:
        copy.wait_send()


def run_filter(psi, cell_ham, proj_table, coupling, kinds):
    blocks = lax.axis_size("cells")
    groups = lax.axis_size("bands")
    side = cube_root(blocks)
    share_of = groups * LANES // blocks
    sum_type = f32 if share_of % 16 else bf16
    slot_rows = (psi.shape[0] ** 3 + 3 * psi.shape[0] ** 2) // groups
    block = psi.shape[0]
    nodes = cell_ham.shape[-1]
    cells = cell_ham.shape[0]
    padded = -(-nodes // LANES) * LANES
    nproj = proj_table.shape[2]
    corner_span = 8 * nproj
    rows = (block + 1) ** 2 * 24
    node_steps, vert_steps = 2 * DEGREE, 2 * DEGREE + 1
    _, node_buffer = message_rows(block, 1)
    _, vert_buffer = message_rows(CPD, nproj)
    vmem = pl.BlockSpec(memory_space=pltpu.VMEM)
    flops = DEGREE * cells * 2 * LANES * nodes * (nodes + 2 * corner_span)
    return pl.pallas_call(
        functools.partial(filter_kernel, blocks, groups, side, nodes),
        out_shape=(
            jax.ShapeDtypeStruct(psi.shape, bf16),
            jax.ShapeDtypeStruct((share_of, LANES), f32),
        ),
        in_specs=[
            vmem,
            pl.BlockSpec(memory_space=pl.ANY),
            vmem,
            vmem,
            pl.BlockSpec(memory_space=pltpu.SMEM),
        ],
        out_specs=(vmem, vmem),
        scratch_shapes=[
            pltpu.VMEM((cells, -(-nodes // 16) * 16, padded), bf16),
            pltpu.VMEM((rows, LANES), f32),
            pltpu.VMEM((rows, LANES), f32),
            pltpu.VMEM((rows, LANES), f32),
            pltpu.VMEM((padded, LANES), f32),
            pltpu.VMEM((cells, padded, LANES), bf16),
            pltpu.VMEM((cells, corner_span, padded), bf16),
            pltpu.VMEM((cells, corner_span, LANES), f32),
            pltpu.VMEM((cells, padded, LANES), f32),
            pltpu.VMEM(((CPD + 1) ** 3, nproj, LANES), f32),
            pltpu.VMEM(((CPD + 1) ** 3, nproj, LANES), f32),
            pltpu.VMEM((node_steps, node_buffer, LANES), bf16),
            pltpu.VMEM((node_steps, node_buffer, LANES), bf16),
            pltpu.VMEM((vert_steps, vert_buffer, LANES), bf16),
            pltpu.VMEM((vert_steps, vert_buffer, LANES), bf16),
            pltpu.SemaphoreType.DMA((node_steps, 7)),
            pltpu.SemaphoreType.DMA((node_steps, 7)),
            pltpu.SemaphoreType.DMA((vert_steps, 7)),
            pltpu.SemaphoreType.DMA((vert_steps, 7)),
            pltpu.SemaphoreType.DMA((1,)),
            pltpu.VMEM((nodes, cells, nodes), bf16),
            pltpu.VMEM((padded // LANES, 16 * cells, LANES), f32),
            pltpu.VMEM((cells, padded, corner_span), bf16),
            pltpu.VMEM((block**3, LANES), bf16),
            pltpu.VMEM((3 * block**2, LANES), bf16),
            pltpu.VMEM((groups, slot_rows, LANES), bf16),
            pltpu.VMEM((slot_rows, groups * LANES), bf16),
            pltpu.VMEM((groups, groups * LANES, LANES), bf16),
            pltpu.VMEM((groups - 1, groups * LANES, LANES), bf16),
            pltpu.VMEM((blocks, share_of, LANES), sum_type),
            pltpu.VMEM((blocks - 1, share_of, LANES), sum_type),
            pltpu.SemaphoreType.DMA((3, groups - 1)),
            pltpu.SemaphoreType.DMA((3, groups - 1)),
            pltpu.SemaphoreType.DMA((2,)),
            pltpu.SemaphoreType.DMA((blocks - 1,)),
            pltpu.SemaphoreType.DMA((blocks - 1,)),
        ],
        compiler_params=pltpu.CompilerParams(
            collective_id=0, has_side_effects=True, vmem_limit_bytes=50 * 1024 * 1024
        ),
        cost_estimate=pl.CostEstimate(
            flops=flops, bytes_accessed=cells * nodes * nodes * 2, transcendentals=0
        ),
    )(psi, jnp.transpose(cell_ham, (1, 0, 2)), proj_table, coupling, kinds)


def local(psi, cell_ham, proj_table, coupling, atom_kind):
    return run_filter(psi, cell_ham, proj_table, coupling, atom_kind)


def solution(mesh):
    in_specs = (
        P("cells", None, None, "bands"),
        P("cells", None, None),
        P(),
        P(),
        P("cells", None, None),
    )
    out_specs = (P("cells", None, None, "bands"), P("cells", "bands"))
    return jax.shard_map(local, mesh=mesh, in_specs=in_specs, out_specs=out_specs, check_vma=False)
```
